32 devices in a mesh: parts: 1, chan: 16 (over z, y, core), tm: 2 (over x), freq: 1.
Axes of the slice: x: 2, y: 2, z: 4, core: 2. Of those that a mesh axis runs over, the one named last changes fastest.
Arguments:
- spectra: bfloat16 [2, 512, 16, 2048], P(None, 'freq', 'tm', ('parts', 'chan')), may hold values from -6 to 6
- owners: int32 [4], P('parts'), may hold values from 0 to 15
- source_rows: int32 [4, 16], P('parts'), may hold values from 0 to 127
Outputs:
- correlations: float32 [4, 16, 2048, 128], P(None, ('tm', 'freq'), ('parts', 'chan'))
The draws below stay inside these ranges and needn't reach their ends.
All inputs are finite; a program needn't handle non-finite values.
Results may differ from the reference program's by a relative error of at most 0.0037.
Values may be sent and summed in bfloat16 or wider, within the bound.
No kernel may reach another device: no remote copies, remote signals or barrier semaphores. Data moves between devices by JAX's collectives and lax.ppermute only.
A program may use at most 64 MiB of HBM per device.

```python
import jax
import jax.numpy as jnp
from jax import lax

FREQ_BINS = 512
WINDOW_LEN = 4096
FIRST_BIN = 64
SOURCES = 16
LAGS = 128
STEPS = 4
C_DEV = 128
CHANNELS = 2048
WINDOWS = 16
SHARDS = 16
N_CHAN = 16


def place_ends(result, key, low, top_value):
    spot = [jax.random.randint(jax.random.fold_in(key, axis), (), 0, length) for axis, length in enumerate(result.shape)]
    main_axis = result.shape.index(max(result.shape))
    next_to = spot[:main_axis] + [(spot[main_axis] + 1) % result.shape[main_axis]] + spot[main_axis + 1:]
    return result.at[tuple(spot)].set(low).at[tuple(next_to)].set(top_value)


def shard_levels(own_key, dims, pieces, smallest, top_value):
    def one(position, parts):
        steps = jax.random.uniform(jax.random.fold_in(jax.random.fold_in(own_key, 6), position), (parts,), jnp.float32, smallest / len(pieces), top_value / len(pieces))
        return jnp.repeat(jnp.exp(steps), dims[position] // parts).reshape((-1,) + (1,) * (len(dims) - position - 1))

    factor_of = one(*pieces[0])
    for cut in pieces[1:]:
        factor_of = factor_of * one(*cut)
    return factor_of


def gaussian(key, extent, width, reach, shards=(), held_as=jnp.bfloat16):
    loudness = shard_levels(key, extent, shards, -0.22, 0.18) if shards else 1.0
    drawn = jax.random.normal(key, extent, jnp.float32) * width * loudness
    return jnp.minimum(jnp.maximum(drawn, -reach), reach).astype(held_as)


def setup_inputs(seed: int = 0, part: int = 0) -> dict:
    streams_of = jax.random.split(jax.random.key(seed), 4)
    part_splits = jax.random.split(jax.random.fold_in(streams_of[3], part), 4)
    return {
        "spectra": gaussian(part_splits[0], (2, FREQ_BINS, WINDOWS, CHANNELS), 1.0, 6.0, ((2, 2), (3, 16))),
        "owners": place_ends(jax.random.randint(part_splits[1], (STEPS,), 0, SHARDS), jax.random.fold_in(part_splits[1], 1), 0, SHARDS - 1).astype(jnp.int32),
        "source_rows": place_ends(jax.random.randint(part_splits[2], (STEPS, SOURCES), 0, C_DEV), jax.random.fold_in(part_splits[2], 1), 0, C_DEV - 1).astype(jnp.int32),
    }


WATER = 0.5

def whiten(block):
    values = block.astype(jnp.float32)
    size = jnp.sqrt(values[0] * values[0] + values[1] * values[1]) + WATER
    return (values / size[None]).astype(jnp.bfloat16)

def make_tables(first_bin, count):
    bins = first_bin + jnp.arange(count, dtype=jnp.int32)
    shifts = jnp.arange(LAGS, dtype=jnp.int32) - LAGS // 2
    phase = jnp.mod(bins[:, None] * shifts[None, :], WINDOW_LEN).astype(jnp.float32)
    angle = phase * (2.0 * 3.141592653589793 / WINDOW_LEN)
    return (jnp.cos(angle), jnp.sin(angle))

def reference(spectra, owners, source_rows):
    chosen = (owners[:, None] * C_DEV + source_rows).reshape(-1).astype(jnp.int32)
    picked = whiten(jnp.take(spectra, chosen, axis=3))
    picked = picked.reshape(2, FREQ_BINS, WINDOWS, STEPS, SOURCES).astype(jnp.float32)
    picked = jnp.transpose(picked, (3, 0, 1, 2, 4))
    flipped = jnp.stack([picked, jnp.stack([-picked[:, 1], picked[:, 0]], axis=1)], axis=1)
    cosine, sine = make_tables(FIRST_BIN, FREQ_BINS)
    hp = lax.Precision.HIGHEST

    def shard_lags(index):
        start = (index * C_DEV).astype(jnp.int32)
        local = lax.dynamic_slice_in_dim(spectra, start, C_DEV, 3)
        local = whiten(local).astype(jnp.float32)
        cross = jnp.einsum('tokfws,kfwc->tofsc', flipped, local, precision=hp)
        lags = jnp.einsum('tfsc,fl->tscl', cross[:, 0], cosine, precision=hp)
        lags = lags - jnp.einsum('tfsc,fl->tscl', cross[:, 1], sine, precision=hp)
        return lags / WINDOWS
    every = lax.map(shard_lags, jnp.arange(N_CHAN, dtype=jnp.int32))
    every = jnp.transpose(every, (1, 2, 0, 3, 4))
    return every.reshape(STEPS, SOURCES, CHANNELS, LAGS)
```

```python
import functools

import jax
import jax.numpy as jnp
import numpy as np
from jax import lax
from jax.experimental import pallas as pl
from jax.experimental.pallas import tpu as pltpu
from jax.sharding import PartitionSpec as P

WINDOW_LEN = 4096
FIRST_BIN = 64
LAGS = 128
RANK = 64
WATER = 0.5
VMEM_LIMIT = 48 * 1024 * 1024

CORE_MASK = 1
HOP_MASKS = (4, 2, 6)
CHUNKS = 8


def lag_basis(bins):
    k = FIRST_BIN + np.arange(bins)
    shifts = np.arange(LAGS) - LAGS // 2
    angle = 2.0 * np.pi * np.mod(k[:, None] * shifts[None, :], WINDOW_LEN) / WINDOW_LEN
    table = np.stack([np.cos(angle), -np.sin(angle)])
    _, _, rows = np.linalg.svd(table.reshape(2 * bins, LAGS), full_matrices=False)
    basis = rows[:RANK]
    return np.einsum("ofl,rl->ofr", table, basis), basis


def chunk_id(index):
    core = index & 1
    second = (index >> 1) & 1
    third = ((index >> 2) ^ (index >> 3)) & 1
    return core * 4 + second * 2 + third


def pick_kernel(place, spectra, onehot, away, home):
    half = pl.program_id(0)
    low = place[0] & 3
    fc = spectra.shape[1] // 4
    gc = away.shape[1]
    win = spectra.shape[2]
    hot = onehot[...]
    for j in range(4):
        first = (low ^ j) * fc
        for k in range(2):
            block = spectra[k, pl.ds(first, fc)].reshape(fc * win, spectra.shape[3])
            got = lax.dot_general(
                hot, block, (((1,), (1,)), ((), ())), preferred_element_type=jnp.float32
            ).astype(jnp.bfloat16)
            for g in range(gc):
                piece = got[:, g * 128 : (g + 1) * 128]

                @pl.when(half == 0)
                def _():
                    away[j, g, k] = piece

                @pl.when(half == 1)
                def _():
                    home[j, g, k] = piece


def pick(place, spectra, onehot):
    bins, win, chans = spectra.shape[1:]
    count = onehot.shape[0]
    gc = bins * win // 128 // CHUNKS
    out = jax.ShapeDtypeStruct((4, gc, 2, count, 128), jnp.bfloat16)
    spec = pl.BlockSpec((4, gc, 2, count, 128), lambda h, place: (0, 0, 0, 0, 0))
    return pl.pallas_call(
        pick_kernel,
        grid_spec=pltpu.PrefetchScalarGridSpec(
            num_scalar_prefetch=1,
            grid=(2,),
            in_specs=[
                pl.BlockSpec((2, bins // 2, win, chans), lambda h, place: (0, (place[0] >> 2) ^ (1 - h), 0, 0)),
                pl.BlockSpec((count, chans), lambda h, place: (0, 0)),
            ],
            out_specs=[spec, spec],
        ),
        out_shape=[out, out],
        compiler_params=pltpu.CompilerParams(vmem_limit_bytes=VMEM_LIMIT),
        cost_estimate=pl.CostEstimate(flops=4 * bins * win * chans * count, bytes_accessed=3 << 20, transcendentals=0),
        name="pick_sources",
    )(place, spectra, onehot)


def whiten_pair(real, imag):
    real = real.astype(jnp.float32)
    imag = imag.astype(jnp.float32)
    size = jnp.sqrt(real * real + imag * imag) + WATER
    return (real / size).astype(jnp.bfloat16), (imag / size).astype(jnp.bfloat16)


def whiten_kernel(place, spectra, out):
    gc = out.shape[1]
    gf = spectra.shape[1] // gc
    for g in range(gc):
        real = spectra[0, g * gf : (g + 1) * gf].reshape(128, 128)
        imag = spectra[1, g * gf : (g + 1) * gf].reshape(128, 128)
        real, imag = whiten_pair(real, imag)
        out[0, g, 0] = real
        out[0, g, 1] = imag


def whiten(place, spectra):
    bins, win, chans = spectra.shape[1:]
    gc = bins * win // 128 // CHUNKS
    return pl.pallas_call(
        whiten_kernel,
        grid_spec=pltpu.PrefetchScalarGridSpec(
            num_scalar_prefetch=1,
            grid=(CHUNKS,),
            in_specs=[pl.BlockSpec((2, bins // CHUNKS, win, chans), lambda p, place: (0, place[0] ^ p, 0, 0))],
            out_specs=pl.BlockSpec((1, gc, 2, 128, 128), lambda p, place: (p, 0, 0, 0, 0)),
        ),
        out_shape=jax.ShapeDtypeStruct((CHUNKS, gc, 2, 128, 128), jnp.bfloat16),
        compiler_params=pltpu.CompilerParams(vmem_limit_bytes=VMEM_LIMIT),
        cost_estimate=pl.CostEstimate(flops=1 << 24, bytes_accessed=4 << 20, transcendentals=1 << 20),
        name="whiten_own",
    )(place, spectra)


def cross_kernel(first, count, *refs):
    sources = refs[:CHUNKS]
    white, table, out, cross = refs[CHUNKS:]
    gc = white.shape[1]
    gf = table.shape[1] // (CHUNKS * 2 * gc)
    win = 128 // gf
    row = lax.broadcasted_iota(jnp.int32, (gf, 128), 0)
    lane = lax.broadcasted_iota(jnp.int32, (gf, 128), 1)
    mask = jnp.where(lane // win == row, 1.0, 0.0).astype(jnp.bfloat16)
    for p in range(CHUNKS):
        source = sources[p]

        def group(g, _):
            wr = white[p, g, 0]
            wi = white[p, g, 1]
            right = jnp.concatenate(
                [jnp.concatenate([wr, wi], axis=1), jnp.concatenate([wi, -wr], axis=1)], axis=0
            )
            sr = source[g, 0, first : first + count].astype(jnp.float32)
            si = source[g, 1, first : first + count].astype(jnp.float32)
            rows = []
            for s in range(count):
                lr = jnp.broadcast_to(sr[s : s + 1], (gf, 128)).astype(jnp.bfloat16) * mask
                li = jnp.broadcast_to(si[s : s + 1], (gf, 128)).astype(jnp.bfloat16) * mask
                rows.append(jnp.concatenate([lr, li], axis=1))
            left = jnp.concatenate(rows, axis=0)
            both = jnp.dot(left, right, preferred_element_type=jnp.float32).astype(jnp.bfloat16)
            at_real = pl.multiple_of(p * 2 * gc * gf + g * gf, gf)
            at_imag = pl.multiple_of((p * 2 + 1) * gc * gf + g * gf, gf)
            for s in range(count):
                cross[pl.ds(at_real, gf), s * 128 : (s + 1) * 128] = both[s * gf : (s + 1) * gf, :128]
                cross[pl.ds(at_imag, gf), s * 128 : (s + 1) * 128] = both[s * gf : (s + 1) * gf, 128:]
            return 0

        lax.fori_loop(0, gc, group, 0)
    left = table[...]
    wide = 512
    for n in range(count * 128 // wide):
        got = jnp.dot(left, cross[:, n * wide : (n + 1) * wide], preferred_element_type=jnp.float32)
        out[:, n * wide : (n + 1) * wide] = got.astype(out.dtype)


def coefficients(sources, white, table, first, count, dtype):
    gc = white.shape[1]
    return pl.pallas_call(
        functools.partial(cross_kernel, first, count),
        in_specs=[pl.BlockSpec(memory_space=pltpu.VMEM)] * (CHUNKS + 2),
        out_specs=pl.BlockSpec(memory_space=pltpu.VMEM),
        out_shape=jax.ShapeDtypeStruct((RANK, count * 128), dtype),
        scratch_shapes=[pltpu.VMEM((table.shape[1], count * 128), jnp.bfloat16)],
        compiler_params=pltpu.CompilerParams(vmem_limit_bytes=VMEM_LIMIT),
        cost_estimate=pl.CostEstimate(
            flops=CHUNKS * gc * count * 16 * 256 * 256 * 2, bytes_accessed=4 << 20, transcendentals=0
        ),
        name="cross_coefficients",
    )(*sources, white, table)


def lags_kernel(own, *refs):
    *others, basis, out = refs
    for s in range(out.shape[0]):
        at = slice(s * 128, (s + 1) * 128)
        value = own[:, at]
        for other in others:
            value = value + other[:, at].astype(jnp.float32)
        high = value.astype(jnp.bfloat16)
        low = (value - high.astype(jnp.float32)).astype(jnp.bfloat16)
        left = jnp.concatenate([high, low, high], axis=0)
        out[s] = lax.dot_general(
            left, basis[...], (((0,), (0,)), ((), ())), preferred_element_type=jnp.float32
        )


def to_lags(own, others, basis):
    count = own.shape[1] // 128
    step = min(8, count)
    block = pl.BlockSpec((RANK, step * 128), lambda s: (0, s))
    return pl.pallas_call(
        lags_kernel,
        grid=(count // step,),
        in_specs=[block] * (1 + len(others)) + [pl.BlockSpec(basis.shape, lambda s: (0, 0))],
        out_specs=pl.BlockSpec((step, 128, LAGS), lambda s: (s, 0, 0)),
        out_shape=jax.ShapeDtypeStruct((count, 128, LAGS), jnp.float32),
        compiler_params=pltpu.CompilerParams(vmem_limit_bytes=VMEM_LIMIT),
        cost_estimate=pl.CostEstimate(flops=count * 128 * 128 * 192 * 2, bytes_accessed=4 << 20, transcendentals=0),
        name="lags",
    )(own, *others, basis)


def spread(away, home, size):
    def across(block, mask):
        return lax.ppermute(block, "chan", [(i, i ^ mask) for i in range(size)])

    half = home + across(away, CORE_MASK)
    parts = [half[j] for j in range(4)]
    total = parts[0]
    for part, mask in zip(parts[1:], HOP_MASKS):
        total = total + across(part, mask)
    for mask in [12] * (size >= 16) + [m for m in (16, 32, 64, 128, 256, 512) if m < size]:
        total = total + across(total, mask)
    real, imag = whiten_pair(total[:, 0], total[:, 1])
    mine = jnp.stack([real, imag], axis=1)
    chunks = [mine] + [across(mine, mask) for mask in HOP_MASKS]
    return chunks + [across(chunk, CORE_MASK) for chunk in chunks]


def per_device(size, spectra, owners, source_rows):
    bins = spectra.shape[1]
    steps, count = source_rows.shape
    shards = lax.axis_size("tm") * lax.axis_size("freq")
    keep = count // shards
    me = lax.axis_index("chan")
    mine = lax.axis_index("tm") * lax.axis_size("freq") + lax.axis_index("freq")
    place = chunk_id(me).reshape(1).astype(jnp.int32)

    shard = jnp.arange(shards, dtype=jnp.int32) ^ mine
    rows = jnp.where(owners[:, None] == me, source_rows, -1).reshape(steps, shards, keep)
    rows = jnp.transpose(jnp.take(rows, shard, axis=1), (1, 0, 2)).reshape(-1)
    onehot = (rows[:, None] == jnp.arange(spectra.shape[3], dtype=jnp.int32)[None, :]).astype(jnp.bfloat16)

    away, home = pick(place, spectra, onehot)
    white = whiten(place, spectra)
    chunks = spread(away, home, size)

    all_bins = bins * lax.axis_size("freq")
    table, basis = lag_basis(all_bins)
    windows = spectra.shape[2] * lax.axis_size("tm")
    table = jnp.asarray((table / windows).astype(jnp.bfloat16))
    table = lax.dynamic_slice_in_dim(table, lax.axis_index("freq") * bins, bins, 1)
    table = table.reshape(2, CHUNKS, bins // CHUNKS, RANK)
    table = jnp.take(table, jnp.arange(CHUNKS, dtype=jnp.int32) ^ place[0], axis=1)
    table = jnp.transpose(table, (3, 1, 0, 2)).reshape(RANK, 2 * bins)

    high = basis.astype(jnp.bfloat16)
    low = (basis - high.astype(np.float64)).astype(jnp.bfloat16)
    basis = jnp.asarray(np.concatenate([high, high, low], axis=0))

    every = steps * keep
    others = []
    for d in range(1, shards):
        part = coefficients(chunks, white, table, d * every, every, jnp.bfloat16)
        others.append(lax.ppermute(part, ("tm", "freq"), [(i, i ^ d) for i in range(shards)]))
    own = coefficients(chunks, white, table, 0, every, jnp.float32)
    out = to_lags(own, others, basis)
    return out.reshape(steps, keep, 128, LAGS)


def solution(mesh):
    placed = (P(None, "freq", "tm", ("parts", "chan")), P("parts"), P("parts", None))
    return jax.shard_map(
        functools.partial(per_device, mesh.shape["chan"]),
        mesh=mesh,
        in_specs=placed,
        out_specs=P(None, ("tm", "freq"), ("parts", "chan"), None),
        check_vma=False,
    )
```

```python
import functools
import math

import jax
import jax.numpy as jnp
import numpy as np
from jax import lax
from jax.experimental import pallas as pl
from jax.experimental.pallas import tpu as pltpu
from jax.sharding import PartitionSpec as P

WINDOW_LEN = 4096
FIRST_BIN = 64
LAGS = 128
RANK = 64
BLOCK = 8
WATER = 0.5
VMEM_LIMIT = 48 * 1024 * 1024

CORE_MASK = 1
HOP_MASKS = (4, 2, 6)
CHUNKS = 8


def chunk_id(index):
    core = index & 1
    second = (index >> 1) & 1
    third = ((index >> 2) ^ (index >> 3)) & 1
    return core * 4 + second * 2 + third


def lag_basis(bins):
    k = FIRST_BIN + np.arange(bins)
    shifts = np.arange(LAGS) - LAGS // 2
    angle = 2.0 * np.pi * np.mod(k[:, None] * shifts[None, :], WINDOW_LEN) / WINDOW_LEN
    table = np.stack([np.cos(angle), -np.sin(angle)])
    _, _, rows = np.linalg.svd(table.reshape(2 * bins, LAGS), full_matrices=False)
    basis = rows[:RANK]
    return np.einsum("ofl,rl->ofr", table, basis), basis


def pick_kernel(shards, side, owners_in, rows_in, spectra, out, owners, rows, staged, sems):
    total = out.shape[3]
    steps = owners.shape[0]
    me = lax.axis_index("chan")
    mine = lax.axis_index("tm") * lax.axis_size("freq") + lax.axis_index("freq")
    place = chunk_id(me)
    scalars = [
        pltpu.make_async_copy(owners_in, owners, sems.at[4]),
        pltpu.make_async_copy(rows_in, rows, sems.at[5]),
    ]
    for copy in scalars:
        copy.start()
    keep = total // (steps * shards)
    fc = staged.shape[2]
    copies = []
    for j in range(4):
        at = pl.multiple_of((place ^ (side + j)) * fc, fc)
        copy = pltpu.make_async_copy(spectra.at[:, pl.ds(at, fc)], staged.at[j], sems.at[j])
        copy.start()
        copies.append(copy)
    for copy in scalars:
        copy.wait()
    sub = lax.broadcasted_iota(jnp.int32, (8, 128), 0)
    lane = lax.broadcasted_iota(jnp.int32, (8, 128), 1)
    hot = []
    for first in range(0, total, 8):
        want = jnp.full((8, 128), -1, jnp.int32)
        for i in range(8):
            d, rest = divmod(first + i, steps * keep)
            t, k = divmod(rest, keep)
            row = jnp.where(owners[t] == me, rows[t, (mine ^ d) * keep + k], -1)
            want = jnp.where(sub == i, row, want)
        hot.append(jnp.where(want == lane, 1.0, 0.0))
    hot = jnp.concatenate(hot, axis=0).astype(jnp.bfloat16)
    for j in range(4):
        copies[j].wait()
        for k in range(2):
            block = staged[j, k].reshape(-1, staged.shape[4])
            got = lax.dot_general(
                hot, block, (((1,), (1,)), ((), ())), preferred_element_type=jnp.float32
            ).astype(jnp.bfloat16)
            for g in range(out.shape[1]):
                out[j, g, k] = got[:, g * 128 : (g + 1) * 128]


def pick(owners, rows, spectra, shards, side):
    bins, win, chans = spectra.shape[1:]
    total = rows.size
    gc = bins * win // 128 // CHUNKS
    return pl.pallas_call(
        functools.partial(pick_kernel, shards, side),
        in_specs=[pl.BlockSpec(memory_space=pl.ANY)] * 3,
        out_specs=pl.BlockSpec(memory_space=pltpu.VMEM),
        out_shape=jax.ShapeDtypeStruct((4, gc, 2, total, 128), jnp.bfloat16),
        scratch_shapes=[
            pltpu.SMEM(owners.shape, jnp.int32),
            pltpu.SMEM(rows.shape, jnp.int32),
            pltpu.VMEM((4, 2, bins // CHUNKS, win, chans), jnp.bfloat16),
            pltpu.SemaphoreType.DMA((6,)),
        ],
        compiler_params=pltpu.CompilerParams(vmem_limit_bytes=VMEM_LIMIT),
        cost_estimate=pl.CostEstimate(
            flops=2 * bins * win * chans * total, bytes_accessed=2 << 20, transcendentals=0
        ),
        name="pick_sources",
    )(owners, rows, spectra)


def whiten_pair(real, imag):
    real = real.astype(jnp.float32)
    imag = imag.astype(jnp.float32)
    size = jnp.sqrt(real * real + imag * imag) + WATER
    return (real / size).astype(jnp.bfloat16), (imag / size).astype(jnp.bfloat16)


def whiten_kernel(meta, spectra, out):
    gc = out.shape[1]
    gf = spectra.shape[1] // gc
    for g in range(gc):
        real = spectra[0, g * gf : (g + 1) * gf].reshape(128, 128)
        imag = spectra[1, g * gf : (g + 1) * gf].reshape(128, 128)
        out[0, g, 0], out[0, g, 1] = whiten_pair(real, imag)


def whiten(meta, spectra):
    bins, win, chans = spectra.shape[1:]
    gc = bins * win // 128 // CHUNKS
    return pl.pallas_call(
        whiten_kernel,
        grid_spec=pltpu.PrefetchScalarGridSpec(
            num_scalar_prefetch=1,
            grid=(CHUNKS,),
            in_specs=[pl.BlockSpec((2, bins // CHUNKS, win, chans), lambda p, meta: (0, meta[0] ^ p, 0, 0))],
            out_specs=pl.BlockSpec((1, gc, 2, 128, 128), lambda p, meta: (p, 0, 0, 0, 0)),
        ),
        out_shape=jax.ShapeDtypeStruct((CHUNKS, gc, 2, 128, 128), jnp.bfloat16),
        compiler_params=pltpu.CompilerParams(vmem_limit_bytes=VMEM_LIMIT),
        cost_estimate=pl.CostEstimate(flops=1 << 24, bytes_accessed=4 << 20, transcendentals=1 << 20),
        name="whiten_block",
    )(meta, spectra)


def cross_kernel(places, first, begun, meta, *refs):
    sources, refs = refs[: len(places)], refs[len(places) :]
    if begun is not None:
        start, *refs = refs
    white, table, out, cross = refs
    count = out.shape[1] // 128
    gc = white.shape[1]
    gf = table.shape[2] // (2 * gc)
    win = 128 // gf
    row = lax.broadcasted_iota(jnp.int32, (gf, 128), 0)
    lane = lax.broadcasted_iota(jnp.int32, (gf, 128), 1)
    mask = jnp.where(lane // win == row, 1.0, 0.0).astype(jnp.bfloat16)
    for i, p in enumerate(places):
        for g in range(gc):
            wr = white[p, g, 0]
            wi = white[p, g, 1]
            right = jnp.concatenate(
                [jnp.concatenate([wr, wi], axis=1), jnp.concatenate([wi, -wr], axis=1)], axis=0
            )
            low = first // 16 * 16
            high = min(-(-(first + count) // 16) * 16, sources[i].shape[2])
            real = sources[i][g, 0, low:high].astype(jnp.float32)[first - low : first - low + count]
            imag = sources[i][g, 1, low:high].astype(jnp.float32)[first - low : first - low + count]
            step = math.gcd(8, count)
            for s0 in range(0, count, step):
                rows = []
                for s in range(s0, s0 + step):
                    lr = jnp.broadcast_to(real[s : s + 1], (gf, 128)).astype(jnp.bfloat16) * mask
                    li = jnp.broadcast_to(imag[s : s + 1], (gf, 128)).astype(jnp.bfloat16) * mask
                    rows.append(jnp.concatenate([lr, li], axis=1))
                left = jnp.concatenate(rows, axis=0)
                both = jnp.dot(left, right, preferred_element_type=jnp.float32).astype(jnp.bfloat16)
                for o in range(2):
                    at = (i * 2 + o) * gc * gf + g * gf
                    for s in range(step):
                        cross[at : at + gf, (s0 + s) * 128 : (s0 + s + 1) * 128] = both[
                            s * gf : (s + 1) * gf, o * 128 : (o + 1) * 128
                        ]
    left = jnp.concatenate([table[meta[0] ^ p] for p in places], axis=1)
    wide = math.gcd(4, count) * 128
    for n in range(count * 128 // wide):
        got = jnp.dot(left, cross[:, n * wide : (n + 1) * wide], preferred_element_type=jnp.float32)
        if begun is not None:
            got = got + start[:, begun * 128 + n * wide : begun * 128 + (n + 1) * wide]
        out[:, n * wide : (n + 1) * wide] = got.astype(out.dtype)


def coefficients(meta, chunks, places, start, white, table, first, count, dtype):
    gc = white.shape[1]
    operands = [chunks[p] for p in places] + ([] if start is None else [start[0]]) + [white, table]
    begun = None if start is None else start[1]
    return pl.pallas_call(
        functools.partial(cross_kernel, places, first, begun),
        in_specs=[pl.BlockSpec(memory_space=pltpu.SMEM)] + [pl.BlockSpec(memory_space=pltpu.VMEM)] * len(operands),
        out_specs=pl.BlockSpec(memory_space=pltpu.VMEM),
        out_shape=jax.ShapeDtypeStruct((RANK, count * 128), dtype),
        scratch_shapes=[pltpu.VMEM((len(places) * table.shape[2], count * 128), jnp.bfloat16)],
        compiler_params=pltpu.CompilerParams(vmem_limit_bytes=VMEM_LIMIT),
        cost_estimate=pl.CostEstimate(
            flops=len(places) * gc * count * 16 * 256 * 256 * 3, bytes_accessed=2 << 20, transcendentals=0
        ),
        name="cross_coefficients",
    )(meta, *operands)


def lags_kernel(own, *refs):
    *others, basis, out, staged, sems = refs
    blocks = sems.shape[0]
    size = out.shape[0] // blocks
    copies = []
    for i in range(blocks):
        for s in range(size):
            at = slice(s * 128, (s + 1) * 128)
            value = own[:, (i * size + s) * 128 : (i * size + s + 1) * 128]
            for other in others[i::blocks]:
                value = value + other[:, at].astype(jnp.float32)
            high = value.astype(jnp.bfloat16)
            low = (value - high.astype(jnp.float32)).astype(jnp.bfloat16)
            left = jnp.concatenate([high, low, high], axis=0)
            staged[i * size + s] = lax.dot_general(
                left, basis[...], (((0,), (0,)), ((), ())), preferred_element_type=jnp.float32
            )
        at = pl.ds(i * size, size)
        copy = pltpu.make_async_copy(staged.at[at], out.at[at], sems.at[i])
        copy.start()
        copies.append(copy)
    for copy in copies:
        copy.wait()


def to_lags(own, others, basis):
    count = own.shape[1] // 128
    operands = [own, *[block for blocks in others for block in blocks], basis]
    shape = (count, 128, LAGS)
    return pl.pallas_call(
        lags_kernel,
        in_specs=[pl.BlockSpec(memory_space=pltpu.VMEM)] * len(operands),
        out_specs=pl.BlockSpec(memory_space=pl.ANY),
        out_shape=jax.ShapeDtypeStruct(shape, jnp.float32),
        scratch_shapes=[pltpu.VMEM(shape, jnp.float32), pltpu.SemaphoreType.DMA((len(others[0]),))],
        compiler_params=pltpu.CompilerParams(vmem_limit_bytes=VMEM_LIMIT),
        cost_estimate=pl.CostEstimate(flops=count * 128 * 128 * 192 * 2, bytes_accessed=1 << 20, transcendentals=0),
        name="lags",
    )(*operands)


def per_device(size, spectra, owners, source_rows):
    bins = spectra.shape[1]
    steps, count = source_rows.shape
    shards = lax.axis_size("tm") * lax.axis_size("freq")
    keep = count // shards
    me = lax.axis_index("chan").astype(jnp.int32)
    meta = chunk_id(me).reshape(1)

    def across(block, mask):
        return lax.ppermute(block, "chan", [(i, i ^ mask) for i in range(size)])

    all_bins = bins * lax.axis_size("freq")
    table, basis = lag_basis(all_bins)
    windows = spectra.shape[2] * lax.axis_size("tm")
    table = jnp.asarray((table / windows).astype(jnp.bfloat16))
    if all_bins != bins:
        table = lax.dynamic_slice_in_dim(table, lax.axis_index("freq") * bins, bins, 1)
    table = jnp.transpose(table.reshape(2, CHUNKS, bins // CHUNKS, RANK), (1, 3, 0, 2)).reshape(CHUNKS, RANK, -1)
    high = basis.astype(jnp.bfloat16)
    low = (basis - high.astype(np.float64)).astype(jnp.bfloat16)
    basis = jnp.asarray(np.concatenate([high, high, low], axis=0))

    inputs = [pltpu.with_memory_space_constraint(x, pltpu.HBM) for x in (owners, source_rows, spectra)]
    away = pick(*inputs, shards, 4)
    home = pick(*inputs, shards, 0)
    half = home + across(away, CORE_MASK)
    half, spectra = lax.optimization_barrier((half, spectra))
    total = half[0]
    arrived = [across(half[j + 1], mask) for j, mask in enumerate(HOP_MASKS)]
    white = whiten(meta, spectra)
    arrived, white = lax.optimization_barrier((arrived, white))
    for part in arrived:
        total = total + part
    for mask in [12] * (size >= 16) + [16 << i for i in range(10) if 16 << i < size]:
        total = total + across(total, mask)
    own = jnp.stack(whiten_pair(total[:, 0], total[:, 1]), axis=1)
    arrived = [across(own, mask) for mask in HOP_MASKS]
    beside = across(own, CORE_MASK)
    begun = coefficients(
        meta, {0: own, 4: beside}, (0, 4), None, white, table, 0, source_rows.size, jnp.float32
    )
    *arrived, begun = lax.optimization_barrier((*arrived, begun))
    chunks = {}
    for j, chunk in enumerate(arrived):
        chunks[j + 1] = chunk
        chunks[j + 5] = across(chunk, CORE_MASK)
    every = steps * keep
    block = min(BLOCK, every)
    firsts = range(0, every, block)
    outer = every * (shards - 1)
    near = coefficients(meta, chunks, (1, 2, 3), (begun, every), white, table, every, outer, jnp.float32)
    sent = {}
    for first in firsts:
        for d in range(1, shards):
            at = d * every + first
            part = coefficients(
                meta, chunks, (5, 6, 7), (near, at - every), white, table, at, block, jnp.bfloat16
            )
            sent[first, d] = lax.ppermute(part, ("tm", "freq"), [(i, i ^ d) for i in range(shards)])
    kept = coefficients(meta, chunks, (1, 2, 3, 5, 6, 7), (begun, 0), white, table, 0, every, jnp.float32)
    others = [[sent[first, d] for first in firsts] for d in range(1, shards)]
    return to_lags(kept, others, basis).reshape(steps, keep, 128, LAGS)


def solution(mesh):
    placed = (P(None, "freq", "tm", ("parts", "chan")), P("parts"), P("parts", None))
    return jax.shard_map(
        functools.partial(per_device, mesh.shape["chan"]),
        mesh=mesh,
        in_specs=placed,
        out_specs=P(None, ("tm", "freq"), ("parts", "chan"), None),
        check_vma=False,
    )
```

```python
import functools
import math

import jax
import jax.numpy as jnp
import numpy as np
from jax import lax
from jax.experimental import pallas as pl
from jax.experimental.pallas import tpu as pltpu
from jax.sharding import PartitionSpec as P

WINDOW_LEN = 4096
FIRST_BIN = 64
LAGS = 128
RANK = 56
LOTS = 2
WATER = 0.5
VMEM_LIMIT = 48 * 1024 * 1024

CORE_MASK = 1
HOP_MASKS = (4, 2, 6)
CHUNKS = 8


def chunk_id(index):
    core = index & 1
    second = (index >> 1) & 1
    third = ((index >> 2) ^ (index >> 3)) & 1
    return core * 4 + second * 2 + third


def lag_basis(bins):
    k = FIRST_BIN + np.arange(bins)
    shifts = np.arange(LAGS) - LAGS // 2
    angle = 2.0 * np.pi * np.mod(k[:, None] * shifts[None, :], WINDOW_LEN) / WINDOW_LEN
    table = np.stack([np.cos(angle), -np.sin(angle)])
    _, _, rows = np.linalg.svd(table.reshape(2 * bins, LAGS), full_matrices=False)
    basis = rows[:RANK]
    return np.einsum("ofl,rl->ofr", table, basis), basis


def pick_kernel(shards, side, owners_in, rows_in, spectra, *refs):
    outs, (owners, rows, staged, sems) = refs[:LOTS], refs[LOTS:]
    steps, count = rows.shape
    keep = count // shards
    few = steps // LOTS
    total = few * count
    me = lax.axis_index("chan")
    mine = lax.axis_index("tm") * lax.axis_size("freq") + lax.axis_index("freq")
    place = chunk_id(me)
    scalars = [
        pltpu.make_async_copy(owners_in, owners, sems.at[4]),
        pltpu.make_async_copy(rows_in, rows, sems.at[5]),
    ]
    for copy in scalars:
        copy.start()
    fc = staged.shape[2]
    copies = []
    for j in range(4):
        at = pl.multiple_of((place ^ (side + j)) * fc, fc)
        copy = pltpu.make_async_copy(spectra.at[:, pl.ds(at, fc)], staged.at[j], sems.at[j])
        copy.start()
        copies.append(copy)
    for copy in scalars:
        copy.wait()
    sub = lax.broadcasted_iota(jnp.int32, (8, 128), 0)
    lane = lax.broadcasted_iota(jnp.int32, (8, 128), 1)
    hot = []
    for first in range(0, LOTS * total, 8):
        want = jnp.full((8, 128), -1, jnp.int32)
        for i in range(8):
            lot, rest = divmod(first + i, total)
            d, rest = divmod(rest, few * keep)
            t, k = divmod(rest, keep)
            t += lot * few
            row = jnp.where(owners[t] == me, rows[t, (mine ^ d) * keep + k], -1)
            want = jnp.where(sub == i, row, want)
        hot.append(jnp.where(want == lane, 1.0, 0.0))
    hot = jnp.concatenate(hot, axis=0).astype(jnp.bfloat16)
    for j in range(4):
        copies[j].wait()
        for k in range(2):
            block = staged[j, k].reshape(-1, staged.shape[4])
            got = lax.dot_general(
                hot, block, (((1,), (1,)), ((), ())), preferred_element_type=jnp.float32
            ).astype(jnp.bfloat16)
            for lot in range(LOTS):
                for g in range(outs[lot].shape[1]):
                    outs[lot][j, g, k] = got[lot * total : (lot + 1) * total, g * 128 : (g + 1) * 128]


def pick(owners, rows, spectra, shards, side):
    bins, win, chans = spectra.shape[1:]
    total = rows.size // LOTS
    gc = bins * win // 128 // CHUNKS
    return pl.pallas_call(
        functools.partial(pick_kernel, shards, side),
        in_specs=[pl.BlockSpec(memory_space=pl.ANY)] * 3,
        out_specs=[pl.BlockSpec(memory_space=pltpu.VMEM)] * LOTS,
        out_shape=[jax.ShapeDtypeStruct((4, gc, 2, total, 128), jnp.bfloat16)] * LOTS,
        scratch_shapes=[
            pltpu.SMEM(owners.shape, jnp.int32),
            pltpu.SMEM(rows.shape, jnp.int32),
            pltpu.VMEM((4, 2, bins // CHUNKS, win, chans), jnp.bfloat16),
            pltpu.SemaphoreType.DMA((6,)),
        ],
        compiler_params=pltpu.CompilerParams(vmem_limit_bytes=VMEM_LIMIT),
        cost_estimate=pl.CostEstimate(
            flops=2 * bins * win * chans * total, bytes_accessed=2 << 20, transcendentals=0
        ),
        name="pick_sources",
    )(owners, rows, spectra)


def whiten_pair(real, imag):
    real = real.astype(jnp.float32)
    imag = imag.astype(jnp.float32)
    size = jnp.sqrt(real * real + imag * imag) + WATER
    return (real / size).astype(jnp.bfloat16), (imag / size).astype(jnp.bfloat16)


def whiten_sum_kernel(left, right, out):
    for g in range(out.shape[0]):
        parts = [left[g, k].astype(jnp.float32) + right[g, k].astype(jnp.float32) for k in range(2)]
        out[g, 0], out[g, 1] = whiten_pair(*parts)


def whiten_sum(left, right):
    return pl.pallas_call(
        whiten_sum_kernel,
        in_specs=[pl.BlockSpec(memory_space=pltpu.VMEM)] * 2,
        out_specs=pl.BlockSpec(memory_space=pltpu.VMEM),
        out_shape=jax.ShapeDtypeStruct(left.shape, left.dtype),
        compiler_params=pltpu.CompilerParams(vmem_limit_bytes=VMEM_LIMIT),
        cost_estimate=pl.CostEstimate(flops=1 << 10, bytes_accessed=1 << 10, transcendentals=0),
        name="whiten_sources",
    )(left, right)


def whiten_kernel(meta, spectra, out):
    gc = out.shape[1]
    gf = spectra.shape[1] // gc
    for g in range(gc):
        real = spectra[0, g * gf : (g + 1) * gf].reshape(128, 128)
        imag = spectra[1, g * gf : (g + 1) * gf].reshape(128, 128)
        out[0, g, 0], out[0, g, 1] = whiten_pair(real, imag)


def whiten(meta, spectra):
    bins, win, chans = spectra.shape[1:]
    gc = bins * win // 128 // CHUNKS
    return pl.pallas_call(
        whiten_kernel,
        grid_spec=pltpu.PrefetchScalarGridSpec(
            num_scalar_prefetch=1,
            grid=(CHUNKS,),
            in_specs=[pl.BlockSpec((2, bins // CHUNKS, win, chans), lambda p, meta: (0, meta[0] ^ p, 0, 0))],
            out_specs=pl.BlockSpec((1, gc, 2, 128, 128), lambda p, meta: (p, 0, 0, 0, 0)),
        ),
        out_shape=jax.ShapeDtypeStruct((CHUNKS, gc, 2, 128, 128), jnp.bfloat16),
        compiler_params=pltpu.CompilerParams(vmem_limit_bytes=VMEM_LIMIT),
        cost_estimate=pl.CostEstimate(flops=1 << 24, bytes_accessed=4 << 20, transcendentals=1 << 20),
        name="whiten_block",
    )(meta, spectra)


def cross_kernel(places, first, begun, behind, meta, *refs):
    groups, refs = refs[: len(places)], refs[len(places) + behind :]
    if begun is not None:
        start, *refs = refs
    white, table, out, cross = refs
    count = out.shape[1] // 128
    gc = white.shape[1]
    gf = table.shape[2] // (2 * gc)
    win = 128 // gf
    row = lax.broadcasted_iota(jnp.int32, (gf, 128), 0)
    lane = lax.broadcasted_iota(jnp.int32, (gf, 128), 1)
    mask = jnp.where(lane // win == row, 1.0, 0.0).astype(jnp.bfloat16)
    low = first // 16 * 16
    high = min(-(-(first + count) // 16) * 16, groups[0].shape[3])
    step = math.gcd(8, count)
    order = [(p, group, n) for place, group in zip(places, groups) for n, p in enumerate(place)]
    for i, (p, group, n) in enumerate(order):
        for g in range(gc):
            wr = white[p, g, 0]
            wi = white[p, g, 1]
            right = jnp.concatenate(
                [jnp.concatenate([wr, wi], axis=1), jnp.concatenate([wi, -wr], axis=1)], axis=0
            )
            real = group[n, g, 0, low:high].astype(jnp.float32)[first - low : first - low + count]
            imag = group[n, g, 1, low:high].astype(jnp.float32)[first - low : first - low + count]
            for s0 in range(0, count, step):
                rows = []
                for s in range(s0, s0 + step):
                    lr = jnp.broadcast_to(real[s : s + 1], (gf, 128)).astype(jnp.bfloat16) * mask
                    li = jnp.broadcast_to(imag[s : s + 1], (gf, 128)).astype(jnp.bfloat16) * mask
                    rows.append(jnp.concatenate([lr, li], axis=1))
                left = jnp.concatenate(rows, axis=0)
                both = jnp.dot(left, right, preferred_element_type=jnp.float32).astype(jnp.bfloat16)
                for o in range(2):
                    at = (i * 2 + o) * gc * gf + g * gf
                    for s in range(step):
                        cross[at : at + gf, (s0 + s) * 128 : (s0 + s + 1) * 128] = both[
                            s * gf : (s + 1) * gf, o * 128 : (o + 1) * 128
                        ]
    left = jnp.concatenate([table[meta[0] ^ p] for p, _, _ in order], axis=1)
    wide = math.gcd(4, count) * 128
    for n in range(count * 128 // wide):
        got = jnp.dot(left, cross[:, n * wide : (n + 1) * wide], preferred_element_type=jnp.float32)
        if begun is not None:
            got = got + start[:, begun * 128 + n * wide : begun * 128 + (n + 1) * wide]
        out[:, n * wide : (n + 1) * wide] = got.astype(out.dtype)


def coefficients(meta, chunks, start, white, table, first, count, dtype, cost=1 << 10, behind=()):
    gc = white.shape[1]
    places = tuple(chunks)
    begun = None if start is None else start[1]
    operands = [*chunks.values(), *behind, *([] if start is None else [start[0]]), white, table]
    whole = pl.BlockSpec(memory_space=pltpu.VMEM)
    return pl.pallas_call(
        functools.partial(cross_kernel, places, first, begun, len(behind)),
        in_specs=[pl.BlockSpec(memory_space=pltpu.SMEM)]
        + [whole] * len(places)
        + [pl.BlockSpec(memory_space=pl.ANY)] * len(behind)
        + [whole] * (len(operands) - len(places) - len(behind)),
        out_specs=whole,
        out_shape=jax.ShapeDtypeStruct((RANK, count * 128), dtype),
        scratch_shapes=[pltpu.VMEM((sum(map(len, places)) * table.shape[2], count * 128), jnp.bfloat16)],
        compiler_params=pltpu.CompilerParams(vmem_limit_bytes=VMEM_LIMIT),
        cost_estimate=pl.CostEstimate(flops=cost, bytes_accessed=1 << 10, transcendentals=0),
        name="cross_coefficients",
    )(meta, *operands)


def lags_kernel(shards, first, *refs):
    own, *others, basis, out, staged, sems = refs[-shards - 4 :]
    count = staged.shape[0]
    step = count // sems.shape[0]
    copies = []
    for s in range(count):
        at = slice(s * 128, (s + 1) * 128)
        value = own[:, at]
        for other in others:
            value = value + other[:, at].astype(jnp.float32)
        high = value.astype(jnp.bfloat16)
        low = (value - high.astype(jnp.float32)).astype(jnp.bfloat16)
        left = jnp.concatenate([high, low, high], axis=0)
        staged[s] = lax.dot_general(
            left, basis[...], (((0,), (0,)), ((), ())), preferred_element_type=jnp.float32
        )
        if (s + 1) % step == 0:
            start = s + 1 - step
            copy = pltpu.make_async_copy(
                staged.at[start : s + 1], out.at[first + start : first + s + 1], sems.at[s // step]
            )
            copy.start()
            copies.append(copy)
    for copy in copies:
        copy.wait()


def to_lags(own, others, basis, lot, done, cost):
    count = own.shape[1] // 128
    operands = [own, *others, basis]
    specs = [pl.BlockSpec(memory_space=pltpu.VMEM)] * len(operands)
    aliases = {}
    if done is not None:
        aliases = {0: 0}
        specs.insert(0, pl.BlockSpec(memory_space=pl.ANY))
        operands.insert(0, done)
    return pl.pallas_call(
        functools.partial(lags_kernel, 1 + len(others), lot * count),
        in_specs=specs,
        out_specs=pl.BlockSpec(memory_space=pl.ANY),
        out_shape=jax.ShapeDtypeStruct((LOTS * count, 128, LAGS), jnp.float32),
        input_output_aliases=aliases,
        scratch_shapes=[
            pltpu.VMEM((count, 128, LAGS), jnp.float32),
            pltpu.SemaphoreType.DMA((count // math.gcd(4, count),)),
        ],
        compiler_params=pltpu.CompilerParams(vmem_limit_bytes=VMEM_LIMIT),
        cost_estimate=pl.CostEstimate(flops=cost, bytes_accessed=1 << 10, transcendentals=0),
        name="lags",
    )(*operands)


def per_device(size, spectra, owners, source_rows):
    bins = spectra.shape[1]
    steps, count = source_rows.shape
    shards = lax.axis_size("tm") * lax.axis_size("freq")
    keep = count // shards
    me = lax.axis_index("chan").astype(jnp.int32)
    meta = chunk_id(me).reshape(1)

    def across(block, mask):
        return lax.ppermute(block, "chan", [(i, i ^ mask) for i in range(size)])

    all_bins = bins * lax.axis_size("freq")
    table, basis = lag_basis(all_bins)
    windows = spectra.shape[2] * lax.axis_size("tm")
    table = jnp.asarray((table / windows).astype(jnp.bfloat16))
    if all_bins != bins:
        table = lax.dynamic_slice_in_dim(table, lax.axis_index("freq") * bins, bins, 1)
    table = jnp.transpose(table.reshape(2, CHUNKS, bins // CHUNKS, RANK), (1, 3, 0, 2)).reshape(CHUNKS, RANK, -1)
    high = basis.astype(jnp.bfloat16)
    low = (basis - high.astype(np.float64)).astype(jnp.bfloat16)
    basis = jnp.asarray(np.concatenate([high, high, low], axis=0))

    inputs = [pltpu.with_memory_space_constraint(x, pltpu.HBM) for x in (owners, source_rows, spectra)]
    away = pick(*inputs, shards, 4)
    home = pick(*inputs, shards, 0)
    lots = range(LOTS)
    halves = [home[i] + across(away[i], CORE_MASK) for i in lots]
    halves[0], spectra = lax.optimization_barrier((halves[0], spectra))
    arrived = [[across(half[j + 1], mask) for j, mask in enumerate(HOP_MASKS)] for half in halves]
    white = whiten(meta, spectra)
    arrived[0], white = lax.optimization_barrier((arrived[0], white))
    totals = []
    for half, parts in zip(halves, arrived):
        total = half[0]
        for part in parts:
            total = total + part
        totals.append(total)
    masks = [16 << i for i in range(10) if 16 << i < size] + [12] * (size >= 16)
    for mask in masks[:-1]:
        totals = [total + across(total, mask) for total in totals]
    others = [across(total, masks[-1]) if masks else jnp.zeros_like(total) for total in totals]
    own = [whiten_sum(total, other) for total, other in zip(totals, others)]
    chunks = [jnp.stack([chunk] + [across(chunk, mask) for mask in HOP_MASKS]) for chunk in own]

    every = steps * keep // LOTS
    near, far = (0, 1, 2, 3), (4, 5, 6, 7)
    out = None
    sent, kept = [], []
    got = []
    for i in lots:
        beside = across(chunks[i], CORE_MASK)
        begun = coefficients(
            meta, {near: chunks[i]}, None, white, table, every, every * (shards - 1), jnp.float32, behind=got
        )
        got = [
            coefficients(meta, {far: beside}, (begun, (d - 1) * every), white, table, d * every, every, jnp.bfloat16)
            for d in range(1, shards)
        ]
        sent.append(
            [
                lax.ppermute(part, ("tm", "freq"), [(m, m ^ (d + 1)) for m in range(shards)])
                for d, part in enumerate(got)
            ]
        )
        kept.append(
            coefficients(meta, {near: chunks[i], far: beside}, None, white, table, 0, every, jnp.float32)
        )
    for i in lots:
        out = to_lags(kept[i], sent[i], basis, i, out, 1 << (10 if i + 1 == LOTS else 30))
    return out.reshape(steps, keep, 128, LAGS)


def solution(mesh):
    placed = (P(None, "freq", "tm", ("parts", "chan")), P("parts"), P("parts", None))
    return jax.shard_map(
        functools.partial(per_device, mesh.shape["chan"]),
        mesh=mesh,
        in_specs=placed,
        out_specs=P(None, ("tm", "freq"), ("parts", "chan"), None),
        check_vma=False,
    )
```

```python
import functools
import math

import jax
import jax.numpy as jnp
import numpy as np
from jax import lax
from jax.experimental import pallas as pl
from jax.experimental.pallas import tpu as pltpu
from jax.sharding import PartitionSpec as P

WINDOW_LEN = 4096
FIRST_BIN = 64
LAGS = 128
RANK = 56
LOTS = 2
WATER = 0.5
VMEM_LIMIT = 48 * 1024 * 1024

CORE_MASK = 1
HOP_MASKS = (4, 2, 6)
CHUNKS = 8


def chunk_id(index):
    core = index & 1
    second = (index >> 1) & 1
    third = ((index >> 2) ^ (index >> 3)) & 1
    return core * 4 + second * 2 + third


def lag_basis(bins):
    k = FIRST_BIN + np.arange(bins)
    shifts = np.arange(LAGS) - LAGS // 2
    angle = 2.0 * np.pi * np.mod(k[:, None] * shifts[None, :], WINDOW_LEN) / WINDOW_LEN
    table = np.stack([np.cos(angle), -np.sin(angle)])
    _, _, rows = np.linalg.svd(table.reshape(2 * bins, LAGS), full_matrices=False)
    basis = rows[:RANK]
    return np.einsum("ofl,rl->ofr", table, basis), basis


def pick_kernel(shards, side, owners_in, rows_in, spectra, *refs):
    outs, (owners, rows, staged, sems) = refs[:LOTS], refs[LOTS:]
    steps, count = rows.shape
    keep = count // shards
    few = steps // LOTS
    total = few * count
    me = lax.axis_index("chan")
    mine = lax.axis_index("tm") * lax.axis_size("freq") + lax.axis_index("freq")
    place = chunk_id(me)
    scalars = [
        pltpu.make_async_copy(owners_in, owners, sems.at[4]),
        pltpu.make_async_copy(rows_in, rows, sems.at[5]),
    ]
    for copy in scalars:
        copy.start()
    fc = staged.shape[2]
    copies = []
    for j in range(4):
        at = pl.multiple_of((place ^ (side + j)) * fc, fc)
        copy = pltpu.make_async_copy(spectra.at[:, pl.ds(at, fc)], staged.at[j], sems.at[j])
        copy.start()
        copies.append(copy)
    for copy in scalars:
        copy.wait()
    sub = lax.broadcasted_iota(jnp.int32, (8, 128), 0)
    lane = lax.broadcasted_iota(jnp.int32, (8, 128), 1)
    hot = []
    for first in range(0, LOTS * total, 8):
        want = jnp.full((8, 128), -1, jnp.int32)
        for i in range(8):
            lot, rest = divmod(first + i, total)
            d, rest = divmod(rest, few * keep)
            t, k = divmod(rest, keep)
            t += lot * few
            row = jnp.where(owners[t] == me, rows[t, (mine ^ d) * keep + k], -1)
            want = jnp.where(sub == i, row, want)
        hot.append(jnp.where(want == lane, 1.0, 0.0))
    hot = jnp.concatenate(hot, axis=0).astype(jnp.bfloat16)
    for j in range(4):
        copies[j].wait()
        for k in range(2):
            block = staged[j, k].reshape(-1, staged.shape[4])
            got = lax.dot_general(
                hot, block, (((1,), (1,)), ((), ())), preferred_element_type=jnp.float32
            ).astype(jnp.bfloat16)
            for lot in range(LOTS):
                for g in range(outs[lot].shape[1]):
                    outs[lot][j, g, k] = got[lot * total : (lot + 1) * total, g * 128 : (g + 1) * 128]


def pick(owners, rows, spectra, shards, side):
    bins, win, chans = spectra.shape[1:]
    total = rows.size // LOTS
    gc = bins * win // 128 // CHUNKS
    return pl.pallas_call(
        functools.partial(pick_kernel, shards, side),
        in_specs=[pl.BlockSpec(memory_space=pl.ANY)] * 3,
        out_specs=[pl.BlockSpec(memory_space=pltpu.VMEM)] * LOTS,
        out_shape=[jax.ShapeDtypeStruct((4, gc, 2, total, 128), jnp.bfloat16)] * LOTS,
        scratch_shapes=[
            pltpu.SMEM(owners.shape, jnp.int32),
            pltpu.SMEM(rows.shape, jnp.int32),
            pltpu.VMEM((4, 2, bins // CHUNKS, win, chans), jnp.bfloat16),
            pltpu.SemaphoreType.DMA((6,)),
        ],
        compiler_params=pltpu.CompilerParams(vmem_limit_bytes=VMEM_LIMIT),
        cost_estimate=pl.CostEstimate(
            flops=2 * bins * win * chans * total, bytes_accessed=2 << 20, transcendentals=0
        ),
        name="pick_sources",
    )(owners, rows, spectra)


def whiten_pair(real, imag):
    real = real.astype(jnp.float32)
    imag = imag.astype(jnp.float32)
    size = jnp.sqrt(real * real + imag * imag) + WATER
    return (real / size).astype(jnp.bfloat16), (imag / size).astype(jnp.bfloat16)


def whiten_sum_kernel(left, right, out):
    for g in range(out.shape[0]):
        parts = [left[g, k].astype(jnp.float32) + right[g, k].astype(jnp.float32) for k in range(2)]
        out[g, 0], out[g, 1] = whiten_pair(*parts)


def whiten_sum(left, right):
    return pl.pallas_call(
        whiten_sum_kernel,
        in_specs=[pl.BlockSpec(memory_space=pltpu.VMEM)] * 2,
        out_specs=pl.BlockSpec(memory_space=pltpu.VMEM),
        out_shape=jax.ShapeDtypeStruct(left.shape, left.dtype),
        compiler_params=pltpu.CompilerParams(vmem_limit_bytes=VMEM_LIMIT),
        cost_estimate=pl.CostEstimate(flops=1 << 10, bytes_accessed=1 << 10, transcendentals=0),
        name="whiten_sources",
    )(left, right)


def whiten_kernel(meta, spectra, out):
    gc = out.shape[1]
    gf = spectra.shape[1] // gc
    for g in range(gc):
        real = spectra[0, g * gf : (g + 1) * gf].reshape(128, 128)
        imag = spectra[1, g * gf : (g + 1) * gf].reshape(128, 128)
        out[0, g, 0], out[0, g, 1] = whiten_pair(real, imag)


def whiten(meta, spectra):
    bins, win, chans = spectra.shape[1:]
    gc = bins * win // 128 // CHUNKS
    return pl.pallas_call(
        whiten_kernel,
        grid_spec=pltpu.PrefetchScalarGridSpec(
            num_scalar_prefetch=1,
            grid=(CHUNKS,),
            in_specs=[pl.BlockSpec((2, bins // CHUNKS, win, chans), lambda p, meta: (0, meta[0] ^ p, 0, 0))],
            out_specs=pl.BlockSpec((1, gc, 2, 128, 128), lambda p, meta: (p, 0, 0, 0, 0)),
        ),
        out_shape=jax.ShapeDtypeStruct((CHUNKS, gc, 2, 128, 128), jnp.bfloat16),
        compiler_params=pltpu.CompilerParams(vmem_limit_bytes=VMEM_LIMIT),
        cost_estimate=pl.CostEstimate(flops=1 << 24, bytes_accessed=4 << 20, transcendentals=1 << 20),
        name="whiten_block",
    )(meta, spectra)


def cross_kernel(places, first, begun, behind, meta, *refs):
    groups, refs = refs[: len(places)], refs[len(places) + behind :]
    if begun is not None:
        start, *refs = refs
    white, table, out, cross = refs
    count = out.shape[1] // 128
    gc = white.shape[1]
    gf = table.shape[2] // (2 * gc)
    win = 128 // gf
    row = lax.broadcasted_iota(jnp.int32, (gf, 128), 0)
    lane = lax.broadcasted_iota(jnp.int32, (gf, 128), 1)
    mask = jnp.where(lane // win == row, 1.0, 0.0).astype(jnp.bfloat16)
    low = first // 16 * 16
    high = min(-(-(first + count) // 16) * 16, groups[0].shape[3])
    step = math.gcd(8, count)
    order = [(p, group, n) for place, group in zip(places, groups) for n, p in enumerate(place)]
    for i, (p, group, n) in enumerate(order):
        for g in range(gc):
            wr = white[p, g, 0]
            wi = white[p, g, 1]
            right = jnp.concatenate(
                [jnp.concatenate([wr, wi], axis=1), jnp.concatenate([wi, -wr], axis=1)], axis=0
            )
            real = group[n, g, 0, low:high].astype(jnp.float32)[first - low : first - low + count]
            imag = group[n, g, 1, low:high].astype(jnp.float32)[first - low : first - low + count]
            for s0 in range(0, count, step):
                rows = []
                for s in range(s0, s0 + step):
                    lr = jnp.broadcast_to(real[s : s + 1], (gf, 128)).astype(jnp.bfloat16) * mask
                    li = jnp.broadcast_to(imag[s : s + 1], (gf, 128)).astype(jnp.bfloat16) * mask
                    rows.append(jnp.concatenate([lr, li], axis=1))
                left = jnp.concatenate(rows, axis=0)
                both = jnp.dot(left, right, preferred_element_type=jnp.float32).astype(jnp.bfloat16)
                for o in range(2):
                    at = (i * 2 + o) * gc * gf + g * gf
                    for s in range(step):
                        cross[at : at + gf, (s0 + s) * 128 : (s0 + s + 1) * 128] = both[
                            s * gf : (s + 1) * gf, o * 128 : (o + 1) * 128
                        ]
    left = jnp.concatenate([table[meta[0] ^ p] for p, _, _ in order], axis=1)
    wide = math.gcd(4, count) * 128
    for n in range(count * 128 // wide):
        got = jnp.dot(left, cross[:, n * wide : (n + 1) * wide], preferred_element_type=jnp.float32)
        if begun is not None:
            got = got + start[:, begun * 128 + n * wide : begun * 128 + (n + 1) * wide]
        out[:, n * wide : (n + 1) * wide] = got.astype(out.dtype)


def coefficients(meta, chunks, start, white, table, first, count, dtype, cost=1 << 10, behind=()):
    gc = white.shape[1]
    places = tuple(chunks)
    begun = None if start is None else start[1]
    operands = [*chunks.values(), *behind, *([] if start is None else [start[0]]), white, table]
    whole = pl.BlockSpec(memory_space=pltpu.VMEM)
    return pl.pallas_call(
        functools.partial(cross_kernel, places, first, begun, len(behind)),
        in_specs=[pl.BlockSpec(memory_space=pltpu.SMEM)]
        + [whole] * len(places)
        + [pl.BlockSpec(memory_space=pl.ANY)] * len(behind)
        + [whole] * (len(operands) - len(places) - len(behind)),
        out_specs=whole,
        out_shape=jax.ShapeDtypeStruct((RANK, count * 128), dtype),
        scratch_shapes=[pltpu.VMEM((sum(map(len, places)) * table.shape[2], count * 128), jnp.bfloat16)],
        compiler_params=pltpu.CompilerParams(vmem_limit_bytes=VMEM_LIMIT),
        cost_estimate=pl.CostEstimate(flops=cost, bytes_accessed=1 << 10, transcendentals=0),
        name="cross_coefficients",
    )(meta, *operands)


def lags_kernel(shards, first, *refs):
    own, *others, basis, out, staged, sems = refs[-shards - 4 :]
    count = staged.shape[0]
    step = count // sems.shape[0]
    copies = []
    for s in range(count):
        at = slice(s * 128, (s + 1) * 128)
        value = own[:, at]
        for other in others:
            value = value + other[:, at].astype(jnp.float32)
        high = value.astype(jnp.bfloat16)
        low = (value - high.astype(jnp.float32)).astype(jnp.bfloat16)
        left = jnp.concatenate([high, low, high], axis=0)
        staged[s] = lax.dot_general(
            left, basis[...], (((0,), (0,)), ((), ())), preferred_element_type=jnp.float32
        )
        if (s + 1) % step == 0:
            start = s + 1 - step
            copy = pltpu.make_async_copy(
                staged.at[start : s + 1], out.at[first + start : first + s + 1], sems.at[s // step]
            )
            copy.start()
            copies.append(copy)
    for copy in copies:
        copy.wait()


def to_lags(own, others, basis, lot, done, cost):
    count = own.shape[1] // 128
    operands = [own, *others, basis]
    specs = [pl.BlockSpec(memory_space=pltpu.VMEM)] * len(operands)
    aliases = {}
    if done is not None:
        aliases = {0: 0}
        specs.insert(0, pl.BlockSpec(memory_space=pl.ANY))
        operands.insert(0, done)
    return pl.pallas_call(
        functools.partial(lags_kernel, 1 + len(others), lot * count),
        in_specs=specs,
        out_specs=pl.BlockSpec(memory_space=pl.ANY),
        out_shape=jax.ShapeDtypeStruct((LOTS * count, 128, LAGS), jnp.float32),
        input_output_aliases=aliases,
        scratch_shapes=[
            pltpu.VMEM((count, 128, LAGS), jnp.float32),
            pltpu.SemaphoreType.DMA((count // math.gcd(4, count),)),
        ],
        compiler_params=pltpu.CompilerParams(vmem_limit_bytes=VMEM_LIMIT),
        cost_estimate=pl.CostEstimate(flops=cost, bytes_accessed=1 << 10, transcendentals=0),
        name="lags",
    )(*operands)


def stack_kernel(count, *refs):
    for i in range(count):
        refs[-1][i] = refs[i][...]


def stack(blocks, behind):
    whole = pl.BlockSpec(memory_space=pltpu.VMEM)
    return pl.pallas_call(
        functools.partial(stack_kernel, len(blocks)),
        in_specs=[whole] * len(blocks) + [pl.BlockSpec(memory_space=pl.ANY)] * len(behind),
        out_specs=whole,
        out_shape=jax.ShapeDtypeStruct((len(blocks), *blocks[0].shape), blocks[0].dtype),
        compiler_params=pltpu.CompilerParams(vmem_limit_bytes=VMEM_LIMIT),
        cost_estimate=pl.CostEstimate(flops=1 << 10, bytes_accessed=1 << 10, transcendentals=0),
        name="stack",
    )(*blocks, *behind)


def per_device(size, spectra, owners, source_rows):
    bins = spectra.shape[1]
    steps, count = source_rows.shape
    shards = lax.axis_size("tm") * lax.axis_size("freq")
    keep = count // shards
    me = lax.axis_index("chan").astype(jnp.int32)
    meta = chunk_id(me).reshape(1)

    def across(block, mask):
        return lax.ppermute(block, "chan", [(i, i ^ mask) for i in range(size)])

    all_bins = bins * lax.axis_size("freq")
    table, basis = lag_basis(all_bins)
    windows = spectra.shape[2] * lax.axis_size("tm")
    table = jnp.asarray((table / windows).astype(jnp.bfloat16))
    if all_bins != bins:
        table = lax.dynamic_slice_in_dim(table, lax.axis_index("freq") * bins, bins, 1)
    table = jnp.transpose(table.reshape(2, CHUNKS, bins // CHUNKS, RANK), (1, 3, 0, 2)).reshape(CHUNKS, RANK, -1)
    high = basis.astype(jnp.bfloat16)
    low = (basis - high.astype(np.float64)).astype(jnp.bfloat16)
    basis = jnp.asarray(np.concatenate([high, high, low], axis=0))

    inputs = [pltpu.with_memory_space_constraint(x, pltpu.HBM) for x in (owners, source_rows, spectra)]
    away = pick(*inputs, shards, 4)
    home = pick(*inputs, shards, 0)
    lots = range(LOTS)
    halves = [home[i] + across(away[i], CORE_MASK) for i in lots]
    halves[0], spectra = lax.optimization_barrier((halves[0], spectra))
    arrived = [[across(half[j + 1], mask) for j, mask in enumerate(HOP_MASKS)] for half in halves]
    white = whiten(meta, spectra)
    arrived[0], white = lax.optimization_barrier((arrived[0], white))
    totals = []
    for half, parts in zip(halves, arrived):
        total = half[0]
        for part in parts:
            total = total + part
        totals.append(total)
    masks = [16 << i for i in range(10) if 16 << i < size] + [12] * (size >= 16)
    for mask in masks[:-1]:
        totals = [total + across(total, mask) for total in totals]
    others = [across(total, masks[-1]) if masks else jnp.zeros_like(total) for total in totals]
    own = [whiten_sum(total, other) for total, other in zip(totals, others)]
    arrived = [[chunk] + [across(chunk, mask) for mask in HOP_MASKS] for chunk in own]

    every = steps * keep // LOTS
    near, far = (0, 1, 2, 3), (4, 5, 6, 7)
    out = None
    sent, kept = [], []
    got = []
    for i in lots:
        chunks = stack(arrived[i], [begun] if i else [])
        beside = across(chunks, CORE_MASK)
        begun = coefficients(
            meta, {near: chunks}, None, white, table, every, every * (shards - 1), jnp.float32
        )
        got = [
            coefficients(meta, {far: beside}, (begun, (d - 1) * every), white, table, d * every, every, jnp.bfloat16)
            for d in range(1, shards)
        ]
        sent.append(
            [
                lax.ppermute(part, ("tm", "freq"), [(m, m ^ (d + 1)) for m in range(shards)])
                for d, part in enumerate(got)
            ]
        )
        kept.append(
            coefficients(meta, {near: chunks, far: beside}, None, white, table, 0, every, jnp.float32)
        )
    for i in lots:
        out = to_lags(kept[i], sent[i], basis, i, out, 1 << (10 if i + 1 == LOTS else 28))
    return out.reshape(steps, keep, 128, LAGS)


def solution(mesh):
    placed = (P(None, "freq", "tm", ("parts", "chan")), P("parts"), P("parts", None))
    return jax.shard_map(
        functools.partial(per_device, mesh.shape["chan"]),
        mesh=mesh,
        in_specs=placed,
        out_specs=P(None, ("tm", "freq"), ("parts", "chan"), None),
        check_vma=False,
    )
```

```python
import functools
import math

import jax
import jax.numpy as jnp
import numpy as np
from jax import lax
from jax.experimental import pallas as pl
from jax.experimental.pallas import tpu as pltpu
from jax.sharding import PartitionSpec as P

WINDOW_LEN = 4096
FIRST_BIN = 64
LAGS = 128
RANK = 56
LOTS = 2
BLOCK = 8
WATER = 0.5
VMEM_LIMIT = 48 * 1024 * 1024

CORE_MASK = 1
HOP_MASKS = (4, 2, 6)
CHUNKS = 8


def chunk_id(index):
    core = index & 1
    second = (index >> 1) & 1
    third = ((index >> 2) ^ (index >> 3)) & 1
    return core * 4 + second * 2 + third


def lag_basis(bins):
    k = FIRST_BIN + np.arange(bins)
    shifts = np.arange(LAGS) - LAGS // 2
    angle = 2.0 * np.pi * np.mod(k[:, None] * shifts[None, :], WINDOW_LEN) / WINDOW_LEN
    table = np.stack([np.cos(angle), -np.sin(angle)])
    _, _, rows = np.linalg.svd(table.reshape(2 * bins, LAGS), full_matrices=False)
    basis = rows[:RANK]
    return np.einsum("ofl,rl->ofr", table, basis), basis


def pick_kernel(shards, side, owners_in, rows_in, spectra, *refs):
    outs, (owners, rows, staged, sems) = refs[:LOTS], refs[LOTS:]
    steps, count = rows.shape
    keep = count // shards
    few = steps // LOTS
    total = few * count
    me = lax.axis_index("chan")
    mine = lax.axis_index("tm") * lax.axis_size("freq") + lax.axis_index("freq")
    place = chunk_id(me)
    scalars = [
        pltpu.make_async_copy(owners_in, owners, sems.at[4]),
        pltpu.make_async_copy(rows_in, rows, sems.at[5]),
    ]
    for copy in scalars:
        copy.start()
    fc = staged.shape[2]
    copies = []
    for j in range(4):
        at = pl.multiple_of((place ^ (side + j)) * fc, fc)
        copy = pltpu.make_async_copy(spectra.at[:, pl.ds(at, fc)], staged.at[j], sems.at[j])
        copy.start()
        copies.append(copy)
    for copy in scalars:
        copy.wait()
    sub = lax.broadcasted_iota(jnp.int32, (8, 128), 0)
    lane = lax.broadcasted_iota(jnp.int32, (8, 128), 1)
    hot = []
    for first in range(0, LOTS * total, 8):
        want = jnp.full((8, 128), -1, jnp.int32)
        for i in range(8):
            lot, rest = divmod(first + i, total)
            d, rest = divmod(rest, few * keep)
            t, k = divmod(rest, keep)
            t += lot * few
            row = jnp.where(owners[t] == me, rows[t, (mine ^ d) * keep + k], -1)
            want = jnp.where(sub == i, row, want)
        hot.append(jnp.where(want == lane, 1.0, 0.0))
    hot = jnp.concatenate(hot, axis=0).astype(jnp.bfloat16)
    for j in range(4):
        copies[j].wait()
        for k in range(2):
            block = staged[j, k].reshape(-1, staged.shape[4])
            got = lax.dot_general(
                hot, block, (((1,), (1,)), ((), ())), preferred_element_type=jnp.float32
            ).astype(jnp.bfloat16)
            for lot in range(LOTS):
                for g in range(outs[lot].shape[1]):
                    outs[lot][j, g, k] = got[lot * total : (lot + 1) * total, g * 128 : (g + 1) * 128]


def pick(owners, rows, spectra, shards, side):
    bins, win, chans = spectra.shape[1:]
    total = rows.size // LOTS
    gc = bins * win // 128 // CHUNKS
    return pl.pallas_call(
        functools.partial(pick_kernel, shards, side),
        in_specs=[pl.BlockSpec(memory_space=pl.ANY)] * 3,
        out_specs=[pl.BlockSpec(memory_space=pltpu.VMEM)] * LOTS,
        out_shape=[jax.ShapeDtypeStruct((4, gc, 2, total, 128), jnp.bfloat16)] * LOTS,
        scratch_shapes=[
            pltpu.SMEM(owners.shape, jnp.int32),
            pltpu.SMEM(rows.shape, jnp.int32),
            pltpu.VMEM((4, 2, bins // CHUNKS, win, chans), jnp.bfloat16),
            pltpu.SemaphoreType.DMA((6,)),
        ],
        compiler_params=pltpu.CompilerParams(vmem_limit_bytes=VMEM_LIMIT),
        cost_estimate=pl.CostEstimate(
            flops=2 * bins * win * chans * total, bytes_accessed=2 << 20, transcendentals=0
        ),
        name="pick_sources",
    )(owners, rows, spectra)


def whiten_pair(real, imag):
    real = real.astype(jnp.float32)
    imag = imag.astype(jnp.float32)
    size = jnp.sqrt(real * real + imag * imag) + WATER
    return (real / size).astype(jnp.bfloat16), (imag / size).astype(jnp.bfloat16)


def whiten_sum_kernel(left, right, out):
    for g in range(out.shape[0]):
        parts = [left[g, k].astype(jnp.float32) + right[g, k].astype(jnp.float32) for k in range(2)]
        out[g, 0], out[g, 1] = whiten_pair(*parts)


def whiten_sum(left, right):
    return pl.pallas_call(
        whiten_sum_kernel,
        in_specs=[pl.BlockSpec(memory_space=pltpu.VMEM)] * 2,
        out_specs=pl.BlockSpec(memory_space=pltpu.VMEM),
        out_shape=jax.ShapeDtypeStruct(left.shape, left.dtype),
        compiler_params=pltpu.CompilerParams(vmem_limit_bytes=VMEM_LIMIT),
        cost_estimate=pl.CostEstimate(flops=1 << 10, bytes_accessed=1 << 10, transcendentals=0),
        name="whiten_sources",
    )(left, right)


def whiten_kernel(meta, spectra, out):
    gc = out.shape[1]
    gf = spectra.shape[1] // gc
    for g in range(gc):
        real = spectra[0, g * gf : (g + 1) * gf].reshape(128, 128)
        imag = spectra[1, g * gf : (g + 1) * gf].reshape(128, 128)
        out[0, g, 0], out[0, g, 1] = whiten_pair(real, imag)


def whiten(meta, spectra):
    bins, win, chans = spectra.shape[1:]
    gc = bins * win // 128 // CHUNKS
    return pl.pallas_call(
        whiten_kernel,
        grid_spec=pltpu.PrefetchScalarGridSpec(
            num_scalar_prefetch=1,
            grid=(CHUNKS,),
            in_specs=[pl.BlockSpec((2, bins // CHUNKS, win, chans), lambda p, meta: (0, meta[0] ^ p, 0, 0))],
            out_specs=pl.BlockSpec((1, gc, 2, 128, 128), lambda p, meta: (p, 0, 0, 0, 0)),
        ),
        out_shape=jax.ShapeDtypeStruct((CHUNKS, gc, 2, 128, 128), jnp.bfloat16),
        compiler_params=pltpu.CompilerParams(vmem_limit_bytes=VMEM_LIMIT),
        cost_estimate=pl.CostEstimate(flops=1 << 24, bytes_accessed=4 << 20, transcendentals=1 << 20),
        name="whiten_block",
    )(meta, spectra)


def cross_kernel(places, first, begun, behind, meta, *refs):
    groups, refs = refs[: len(places)], refs[len(places) + behind :]
    if begun is not None:
        start, *refs = refs
    white, table, out, cross = refs
    count = out.shape[1] // 128
    gc = white.shape[1]
    gf = table.shape[2] // (2 * gc)
    win = 128 // gf
    row = lax.broadcasted_iota(jnp.int32, (gf, 128), 0)
    lane = lax.broadcasted_iota(jnp.int32, (gf, 128), 1)
    mask = jnp.where(lane // win == row, 1.0, 0.0).astype(jnp.bfloat16)
    low = first // 16 * 16
    high = min(-(-(first + count) // 16) * 16, groups[0].shape[3])
    step = math.gcd(8, count)
    order = [(p, group, n) for place, group in zip(places, groups) for n, p in enumerate(place)]
    for i, (p, group, n) in enumerate(order):
        for g in range(gc):
            wr = white[p, g, 0]
            wi = white[p, g, 1]
            right = jnp.concatenate(
                [jnp.concatenate([wr, wi], axis=1), jnp.concatenate([wi, -wr], axis=1)], axis=0
            )
            real = group[n, g, 0, low:high].astype(jnp.float32)[first - low : first - low + count]
            imag = group[n, g, 1, low:high].astype(jnp.float32)[first - low : first - low + count]
            for s0 in range(0, count, step):
                rows = []
                for s in range(s0, s0 + step):
                    lr = jnp.broadcast_to(real[s : s + 1], (gf, 128)).astype(jnp.bfloat16) * mask
                    li = jnp.broadcast_to(imag[s : s + 1], (gf, 128)).astype(jnp.bfloat16) * mask
                    rows.append(jnp.concatenate([lr, li], axis=1))
                left = jnp.concatenate(rows, axis=0)
                both = jnp.dot(left, right, preferred_element_type=jnp.float32).astype(jnp.bfloat16)
                for o in range(2):
                    at = (i * 2 + o) * gc * gf + g * gf
                    for s in range(step):
                        cross[at : at + gf, (s0 + s) * 128 : (s0 + s + 1) * 128] = both[
                            s * gf : (s + 1) * gf, o * 128 : (o + 1) * 128
                        ]
    left = jnp.concatenate([table[meta[0] ^ p] for p, _, _ in order], axis=1)
    wide = math.gcd(4, count) * 128
    for n in range(count * 128 // wide):
        got = jnp.dot(left, cross[:, n * wide : (n + 1) * wide], preferred_element_type=jnp.float32)
        if begun is not None:
            got = got + start[:, begun * 128 + n * wide : begun * 128 + (n + 1) * wide]
        out[:, n * wide : (n + 1) * wide] = got.astype(out.dtype)


def coefficients(meta, chunks, start, white, table, first, count, dtype, cost=1 << 10, behind=()):
    gc = white.shape[1]
    places = tuple(chunks)
    begun = None if start is None else start[1]
    operands = [*chunks.values(), *behind, *([] if start is None else [start[0]]), white, table]
    whole = pl.BlockSpec(memory_space=pltpu.VMEM)
    return pl.pallas_call(
        functools.partial(cross_kernel, places, first, begun, len(behind)),
        in_specs=[pl.BlockSpec(memory_space=pltpu.SMEM)]
        + [whole] * len(places)
        + [pl.BlockSpec(memory_space=pl.ANY)] * len(behind)
        + [whole] * (len(operands) - len(places) - len(behind)),
        out_specs=whole,
        out_shape=jax.ShapeDtypeStruct((RANK, count * 128), dtype),
        scratch_shapes=[pltpu.VMEM((sum(map(len, places)) * table.shape[2], count * 128), jnp.bfloat16)],
        compiler_params=pltpu.CompilerParams(vmem_limit_bytes=VMEM_LIMIT),
        cost_estimate=pl.CostEstimate(flops=cost, bytes_accessed=1 << 10, transcendentals=0),
        name="cross_coefficients",
    )(meta, *operands)


def lags_kernel(blocks, first, skip, *refs):
    *inputs, out, staged, sems = refs
    own, *others, basis = inputs[len(inputs) - 2 - blocks[0] * blocks[1] :]
    count = staged.shape[0]
    size = count // blocks[0]
    step = count // sems.shape[0]
    copies = []
    for s in range(count):
        at = slice(s % size * 128, (s % size + 1) * 128)
        value = own[:, (skip + s) * 128 : (skip + s + 1) * 128]
        for other in others[s // size * blocks[1] : (s // size + 1) * blocks[1]]:
            value = value + other[:, at].astype(jnp.float32)
        high = value.astype(jnp.bfloat16)
        low = (value - high.astype(jnp.float32)).astype(jnp.bfloat16)
        left = jnp.concatenate([high, low, high], axis=0)
        staged[s] = lax.dot_general(
            left, basis[...], (((0,), (0,)), ((), ())), preferred_element_type=jnp.float32
        )
        if (s + 1) % step == 0:
            start = s + 1 - step
            copy = pltpu.make_async_copy(
                staged.at[start : s + 1], out.at[first + start : first + s + 1], sems.at[s // step]
            )
            copy.start()
            copies.append(copy)
    for copy in copies:
        copy.wait()


def to_lags(own, blocks, basis, first, skip, total, done, cost):
    count = len(blocks) * blocks[0][0].shape[1] // 128
    operands = [own, *[part for block in blocks for part in block], basis]
    specs = [pl.BlockSpec(memory_space=pltpu.VMEM)] * len(operands)
    aliases = {}
    if done is not None:
        aliases = {0: 0}
        specs.insert(0, pl.BlockSpec(memory_space=pl.ANY))
        operands.insert(0, done)
    return pl.pallas_call(
        functools.partial(lags_kernel, (len(blocks), len(blocks[0])), first, skip),
        in_specs=specs,
        out_specs=pl.BlockSpec(memory_space=pl.ANY),
        out_shape=jax.ShapeDtypeStruct((total, 128, LAGS), jnp.float32),
        input_output_aliases=aliases,
        scratch_shapes=[
            pltpu.VMEM((count, 128, LAGS), jnp.float32),
            pltpu.SemaphoreType.DMA((count // math.gcd(4, count),)),
        ],
        compiler_params=pltpu.CompilerParams(vmem_limit_bytes=VMEM_LIMIT),
        cost_estimate=pl.CostEstimate(flops=cost, bytes_accessed=1 << 10, transcendentals=0),
        name="lags",
    )(*operands)


def stack_kernel(count, *refs):
    for i in range(count):
        refs[-1][i] = refs[i][...]


def stack(blocks, behind):
    whole = pl.BlockSpec(memory_space=pltpu.VMEM)
    return pl.pallas_call(
        functools.partial(stack_kernel, len(blocks)),
        in_specs=[whole] * len(blocks) + [pl.BlockSpec(memory_space=pl.ANY)] * len(behind),
        out_specs=whole,
        out_shape=jax.ShapeDtypeStruct((len(blocks), *blocks[0].shape), blocks[0].dtype),
        compiler_params=pltpu.CompilerParams(vmem_limit_bytes=VMEM_LIMIT),
        cost_estimate=pl.CostEstimate(flops=1 << 10, bytes_accessed=1 << 10, transcendentals=0),
        name="stack",
    )(*blocks, *behind)


def per_device(size, spectra, owners, source_rows):
    bins = spectra.shape[1]
    steps, count = source_rows.shape
    shards = lax.axis_size("tm") * lax.axis_size("freq")
    keep = count // shards
    me = lax.axis_index("chan").astype(jnp.int32)
    meta = chunk_id(me).reshape(1)

    def across(block, mask):
        return lax.ppermute(block, "chan", [(i, i ^ mask) for i in range(size)])

    all_bins = bins * lax.axis_size("freq")
    table, basis = lag_basis(all_bins)
    windows = spectra.shape[2] * lax.axis_size("tm")
    table = jnp.asarray((table / windows).astype(jnp.bfloat16))
    if all_bins != bins:
        table = lax.dynamic_slice_in_dim(table, lax.axis_index("freq") * bins, bins, 1)
    table = jnp.transpose(table.reshape(2, CHUNKS, bins // CHUNKS, RANK), (1, 3, 0, 2)).reshape(CHUNKS, RANK, -1)
    high = basis.astype(jnp.bfloat16)
    low = (basis - high.astype(np.float64)).astype(jnp.bfloat16)
    basis = jnp.asarray(np.concatenate([high, high, low], axis=0))

    inputs = [pltpu.with_memory_space_constraint(x, pltpu.HBM) for x in (owners, source_rows, spectra)]
    away = pick(*inputs, shards, 4)
    home = pick(*inputs, shards, 0)
    lots = range(LOTS)
    halves = [home[i] + across(away[i], CORE_MASK) for i in lots]
    halves[0], spectra = lax.optimization_barrier((halves[0], spectra))
    arrived = [[across(half[j + 1], mask) for j, mask in enumerate(HOP_MASKS)] for half in halves]
    white = whiten(meta, spectra)
    arrived[0], white = lax.optimization_barrier((arrived[0], white))
    totals = []
    for half, parts in zip(halves, arrived):
        total = half[0]
        for part in parts:
            total = total + part
        totals.append(total)
    masks = [16 << i for i in range(10) if 16 << i < size] + [12] * (size >= 16)
    for mask in masks[:-1]:
        totals = [total + across(total, mask) for total in totals]
    others = [across(total, masks[-1]) if masks else jnp.zeros_like(total) for total in totals]
    own = [whiten_sum(total, other) for total, other in zip(totals, others)]
    arrived = [[chunk] + [across(chunk, mask) for mask in HOP_MASKS] for chunk in own]

    every = steps * keep // LOTS
    block = math.gcd(BLOCK, every)
    near, far = (0, 1, 2, 3), (4, 5, 6, 7)
    out = None
    sent, kept = [], []
    for i in lots:
        chunks = stack(arrived[i], [begun] if i else [])
        beside = across(chunks, CORE_MASK)
        low = 0 if i + 1 < LOTS else every
        begun = coefficients(meta, {near: chunks}, None, white, table, low, every * shards - low, jnp.float32)
        blocks = []
        for first in range(0, every, block):
            got = [
                coefficients(
                    meta, {far: beside}, (begun, d * every + first - low), white, table, d * every + first, block,
                    jnp.bfloat16,
                )
                for d in range(1, shards)
            ]
            blocks.append(
                [
                    lax.ppermute(part, ("tm", "freq"), [(m, m ^ (d + 1)) for m in range(shards)])
                    for d, part in enumerate(got)
                ]
            )
        sent.append(blocks)
        if low:
            own = coefficients(meta, {near: chunks, far: beside}, None, white, table, 0, every, jnp.float32)
        else:
            own = coefficients(meta, {far: beside}, (begun, 0), white, table, 0, every, jnp.float32)
        kept.append(own)
    for i in lots:
        size = every if i + 1 < LOTS else block
        for first in range(0, every, size):
            some = sent[i][first // block : (first + size) // block]
            out = to_lags(kept[i], some, basis, i * every + first, first, every * LOTS, out, 1 << 28)
    return out.reshape(steps, keep, 128, LAGS)


def solution(mesh):
    placed = (P(None, "freq", "tm", ("parts", "chan")), P("parts"), P("parts", None))
    return jax.shard_map(
        functools.partial(per_device, mesh.shape["chan"]),
        mesh=mesh,
        in_specs=placed,
        out_specs=P(None, ("tm", "freq"), ("parts", "chan"), None),
        check_vma=False,
    )
```

```python
import functools
import math

import jax
import jax.numpy as jnp
import numpy as np
from jax import lax
from jax.experimental import pallas as pl
from jax.experimental.pallas import tpu as pltpu
from jax.sharding import PartitionSpec as P

WINDOW_LEN = 4096
FIRST_BIN = 64
LAGS = 128
RANK = 56
LOTS = 2
BLOCK = 8
WATER = 0.5
VMEM_LIMIT = 48 * 1024 * 1024

CORE_MASK = 1
HOP_MASKS = (4, 2, 6)
CHUNKS = 8


def chunk_id(index):
    core = index & 1
    second = (index >> 1) & 1
    third = ((index >> 2) ^ (index >> 3)) & 1
    return core * 4 + second * 2 + third


def lag_basis(bins):
    k = FIRST_BIN + np.arange(bins)
    shifts = np.arange(LAGS) - LAGS // 2
    angle = 2.0 * np.pi * np.mod(k[:, None] * shifts[None, :], WINDOW_LEN) / WINDOW_LEN
    table = np.stack([np.cos(angle), -np.sin(angle)])
    _, _, rows = np.linalg.svd(table.reshape(2 * bins, LAGS), full_matrices=False)
    basis = rows[:RANK]
    return np.einsum("ofl,rl->ofr", table, basis), basis


def pick_kernel(shards, side, owners_in, rows_in, spectra, *refs):
    outs, (owners, rows, staged, sems) = refs[:LOTS], refs[LOTS:]
    steps, count = rows.shape
    keep = count // shards
    few = steps // LOTS
    total = few * count
    me = lax.axis_index("chan")
    mine = lax.axis_index("tm") * lax.axis_size("freq") + lax.axis_index("freq")
    place = chunk_id(me)
    scalars = [
        pltpu.make_async_copy(owners_in, owners, sems.at[4]),
        pltpu.make_async_copy(rows_in, rows, sems.at[5]),
    ]
    for copy in scalars:
        copy.start()
    fc = staged.shape[2]
    copies = []
    for j in range(4):
        at = pl.multiple_of((place ^ (side + j)) * fc, fc)
        copy = pltpu.make_async_copy(spectra.at[:, pl.ds(at, fc)], staged.at[j], sems.at[j])
        copy.start()
        copies.append(copy)
    for copy in scalars:
        copy.wait()
    sub = lax.broadcasted_iota(jnp.int32, (8, 128), 0)
    lane = lax.broadcasted_iota(jnp.int32, (8, 128), 1)
    hot = []
    for first in range(0, LOTS * total, 8):
        want = jnp.full((8, 128), -1, jnp.int32)
        for i in range(8):
            lot, rest = divmod(first + i, total)
            d, rest = divmod(rest, few * keep)
            t, k = divmod(rest, keep)
            t += lot * few
            row = jnp.where(owners[t] == me, rows[t, (mine ^ d) * keep + k], -1)
            want = jnp.where(sub == i, row, want)
        hot.append(jnp.where(want == lane, 1.0, 0.0))
    hot = jnp.concatenate(hot, axis=0).astype(jnp.bfloat16)
    for j in range(4):
        copies[j].wait()
        for k in range(2):
            block = staged[j, k].reshape(-1, staged.shape[4])
            got = lax.dot_general(
                hot, block, (((1,), (1,)), ((), ())), preferred_element_type=jnp.float32
            ).astype(jnp.bfloat16)
            for lot in range(LOTS):
                for g in range(outs[lot].shape[1]):
                    outs[lot][j, g, k] = got[lot * total : (lot + 1) * total, g * 128 : (g + 1) * 128]


def pick(owners, rows, spectra, shards, side):
    bins, win, chans = spectra.shape[1:]
    total = rows.size // LOTS
    gc = bins * win // 128 // CHUNKS
    return pl.pallas_call(
        functools.partial(pick_kernel, shards, side),
        in_specs=[pl.BlockSpec(memory_space=pl.ANY)] * 3,
        out_specs=[pl.BlockSpec(memory_space=pltpu.VMEM)] * LOTS,
        out_shape=[jax.ShapeDtypeStruct((4, gc, 2, total, 128), jnp.bfloat16)] * LOTS,
        scratch_shapes=[
            pltpu.SMEM(owners.shape, jnp.int32),
            pltpu.SMEM(rows.shape, jnp.int32),
            pltpu.VMEM((4, 2, bins // CHUNKS, win, chans), jnp.bfloat16),
            pltpu.SemaphoreType.DMA((6,)),
        ],
        compiler_params=pltpu.CompilerParams(vmem_limit_bytes=VMEM_LIMIT),
        cost_estimate=pl.CostEstimate(
            flops=2 * bins * win * chans * total, bytes_accessed=2 << 20, transcendentals=0
        ),
        name="pick_sources",
    )(owners, rows, spectra)


def whiten_pair(real, imag):
    real = real.astype(jnp.float32)
    imag = imag.astype(jnp.float32)
    size = jnp.sqrt(real * real + imag * imag) + WATER
    return (real / size).astype(jnp.bfloat16), (imag / size).astype(jnp.bfloat16)


def whiten_sum_kernel(left, right, out):
    for g in range(out.shape[0]):
        parts = [left[g, k].astype(jnp.float32) + right[g, k].astype(jnp.float32) for k in range(2)]
        out[g, 0], out[g, 1] = whiten_pair(*parts)


def whiten_sum(left, right):
    return pl.pallas_call(
        whiten_sum_kernel,
        in_specs=[pl.BlockSpec(memory_space=pltpu.VMEM)] * 2,
        out_specs=pl.BlockSpec(memory_space=pltpu.VMEM),
        out_shape=jax.ShapeDtypeStruct(left.shape, left.dtype),
        compiler_params=pltpu.CompilerParams(vmem_limit_bytes=VMEM_LIMIT),
        cost_estimate=pl.CostEstimate(flops=1 << 10, bytes_accessed=1 << 10, transcendentals=0),
        name="whiten_sources",
    )(left, right)


def whiten_kernel(meta, spectra, out):
    gc = out.shape[1]
    gf = spectra.shape[1] // gc
    for g in range(gc):
        real = spectra[0, g * gf : (g + 1) * gf].reshape(128, 128)
        imag = spectra[1, g * gf : (g + 1) * gf].reshape(128, 128)
        out[0, g, 0], out[0, g, 1] = whiten_pair(real, imag)


def whiten(meta, spectra):
    bins, win, chans = spectra.shape[1:]
    gc = bins * win // 128 // CHUNKS
    return pl.pallas_call(
        whiten_kernel,
        grid_spec=pltpu.PrefetchScalarGridSpec(
            num_scalar_prefetch=1,
            grid=(CHUNKS,),
            in_specs=[pl.BlockSpec((2, bins // CHUNKS, win, chans), lambda p, meta: (0, meta[0] ^ p, 0, 0))],
            out_specs=pl.BlockSpec((1, gc, 2, 128, 128), lambda p, meta: (p, 0, 0, 0, 0)),
        ),
        out_shape=jax.ShapeDtypeStruct((CHUNKS, gc, 2, 128, 128), jnp.bfloat16),
        compiler_params=pltpu.CompilerParams(vmem_limit_bytes=VMEM_LIMIT),
        cost_estimate=pl.CostEstimate(flops=1 << 24, bytes_accessed=4 << 20, transcendentals=1 << 20),
        name="whiten_block",
    )(meta, spectra)


def cross_kernel(places, first, begun, behind, meta, *refs):
    groups, refs = refs[: len(places)], refs[len(places) + behind :]
    if begun is not None:
        start, *refs = refs
    white, table, out, cross = refs
    count = out.shape[1] // 128
    gc = white.shape[1]
    gf = table.shape[2] // (2 * gc)
    win = 128 // gf
    row = lax.broadcasted_iota(jnp.int32, (gf, 128), 0)
    lane = lax.broadcasted_iota(jnp.int32, (gf, 128), 1)
    mask = jnp.where(lane // win == row, 1.0, 0.0).astype(jnp.bfloat16)
    low = first // 16 * 16
    high = min(-(-(first + count) // 16) * 16, groups[0].shape[3])
    step = math.gcd(8, count)
    order = [(p, group, n) for place, group in zip(places, groups) for n, p in enumerate(place)]
    for i, (p, group, n) in enumerate(order):
        for g in range(gc):
            wr = white[p, g, 0]
            wi = white[p, g, 1]
            right = jnp.concatenate(
                [jnp.concatenate([wr, wi], axis=1), jnp.concatenate([wi, -wr], axis=1)], axis=0
            )
            real = group[n, g, 0, low:high].astype(jnp.float32)[first - low : first - low + count]
            imag = group[n, g, 1, low:high].astype(jnp.float32)[first - low : first - low + count]
            for s0 in range(0, count, step):
                rows = []
                for s in range(s0, s0 + step):
                    lr = jnp.broadcast_to(real[s : s + 1], (gf, 128)).astype(jnp.bfloat16) * mask
                    li = jnp.broadcast_to(imag[s : s + 1], (gf, 128)).astype(jnp.bfloat16) * mask
                    rows.append(jnp.concatenate([lr, li], axis=1))
                left = jnp.concatenate(rows, axis=0)
                both = jnp.dot(left, right, preferred_element_type=jnp.float32).astype(jnp.bfloat16)
                for o in range(2):
                    at = (i * 2 + o) * gc * gf + g * gf
                    for s in range(step):
                        cross[at : at + gf, (s0 + s) * 128 : (s0 + s + 1) * 128] = both[
                            s * gf : (s + 1) * gf, o * 128 : (o + 1) * 128
                        ]
    left = jnp.concatenate([table[meta[0] ^ p] for p, _, _ in order], axis=1)
    wide = math.gcd(4, count) * 128
    for n in range(count * 128 // wide):
        got = jnp.dot(left, cross[:, n * wide : (n + 1) * wide], preferred_element_type=jnp.float32)
        if begun is not None:
            got = got + start[:, begun * 128 + n * wide : begun * 128 + (n + 1) * wide]
        out[:, n * wide : (n + 1) * wide] = got.astype(out.dtype)


def coefficients(meta, chunks, start, white, table, first, count, dtype, cost=1 << 10, behind=()):
    gc = white.shape[1]
    places = tuple(chunks)
    begun = None if start is None else start[1]
    operands = [*chunks.values(), *behind, *([] if start is None else [start[0]]), white, table]
    whole = pl.BlockSpec(memory_space=pltpu.VMEM)
    return pl.pallas_call(
        functools.partial(cross_kernel, places, first, begun, len(behind)),
        in_specs=[pl.BlockSpec(memory_space=pltpu.SMEM)]
        + [whole] * len(places)
        + [pl.BlockSpec(memory_space=pl.ANY)] * len(behind)
        + [whole] * (len(operands) - len(places) - len(behind)),
        out_specs=whole,
        out_shape=jax.ShapeDtypeStruct((RANK, count * 128), dtype),
        scratch_shapes=[pltpu.VMEM((sum(map(len, places)) * table.shape[2], count * 128), jnp.bfloat16)],
        compiler_params=pltpu.CompilerParams(vmem_limit_bytes=VMEM_LIMIT),
        cost_estimate=pl.CostEstimate(flops=cost, bytes_accessed=1 << 10, transcendentals=0),
        name="cross_coefficients",
    )(meta, *operands)


def lags_kernel(blocks, first, skip, *refs):
    *inputs, out, staged, sems = refs
    own, *others, basis = inputs[len(inputs) - 2 - blocks[0] * blocks[1] :]
    count = staged.shape[0]
    size = count // blocks[0]
    step = count // sems.shape[0]
    copies = []
    for s in range(count):
        at = slice(s % size * 128, (s % size + 1) * 128)
        value = own[:, (skip + s) * 128 : (skip + s + 1) * 128]
        for other in others[s // size * blocks[1] : (s // size + 1) * blocks[1]]:
            value = value + other[:, at].astype(jnp.float32)
        high = value.astype(jnp.bfloat16)
        low = (value - high.astype(jnp.float32)).astype(jnp.bfloat16)
        left = jnp.concatenate([high, low, high], axis=0)
        staged[s] = lax.dot_general(
            left, basis[...], (((0,), (0,)), ((), ())), preferred_element_type=jnp.float32
        )
        if (s + 1) % step == 0:
            start = s + 1 - step
            copy = pltpu.make_async_copy(
                staged.at[start : s + 1], out.at[first + start : first + s + 1], sems.at[s // step]
            )
            copy.start()
            copies.append(copy)
    for copy in copies:
        copy.wait()


def to_lags(own, blocks, basis, first, skip, total, done, cost):
    count = len(blocks) * blocks[0][0].shape[1] // 128
    operands = [own, *[part for block in blocks for part in block], basis]
    specs = [pl.BlockSpec(memory_space=pltpu.VMEM)] * len(operands)
    aliases = {}
    if done is not None:
        aliases = {0: 0}
        specs.insert(0, pl.BlockSpec(memory_space=pl.ANY))
        operands.insert(0, done)
    return pl.pallas_call(
        functools.partial(lags_kernel, (len(blocks), len(blocks[0])), first, skip),
        in_specs=specs,
        out_specs=pl.BlockSpec(memory_space=pl.ANY),
        out_shape=jax.ShapeDtypeStruct((total, 128, LAGS), jnp.float32),
        input_output_aliases=aliases,
        scratch_shapes=[
            pltpu.VMEM((count, 128, LAGS), jnp.float32),
            pltpu.SemaphoreType.DMA((count // math.gcd(2, count),)),
        ],
        compiler_params=pltpu.CompilerParams(vmem_limit_bytes=VMEM_LIMIT),
        cost_estimate=pl.CostEstimate(flops=cost, bytes_accessed=1 << 10, transcendentals=0),
        name="lags",
    )(*operands)


def stack_kernel(count, *refs):
    for i in range(count):
        refs[-1][i] = refs[i][...]


def stack(blocks, behind):
    whole = pl.BlockSpec(memory_space=pltpu.VMEM)
    return pl.pallas_call(
        functools.partial(stack_kernel, len(blocks)),
        in_specs=[whole] * len(blocks) + [pl.BlockSpec(memory_space=pl.ANY)] * len(behind),
        out_specs=whole,
        out_shape=jax.ShapeDtypeStruct((len(blocks), *blocks[0].shape), blocks[0].dtype),
        compiler_params=pltpu.CompilerParams(vmem_limit_bytes=VMEM_LIMIT),
        cost_estimate=pl.CostEstimate(flops=1 << 10, bytes_accessed=1 << 10, transcendentals=0),
        name="stack",
    )(*blocks, *behind)


def per_device(size, spectra, owners, source_rows):
    bins = spectra.shape[1]
    steps, count = source_rows.shape
    shards = lax.axis_size("tm") * lax.axis_size("freq")
    keep = count // shards
    me = lax.axis_index("chan").astype(jnp.int32)
    meta = chunk_id(me).reshape(1)

    def across(block, mask):
        return lax.ppermute(block, "chan", [(i, i ^ mask) for i in range(size)])

    all_bins = bins * lax.axis_size("freq")
    table, basis = lag_basis(all_bins)
    windows = spectra.shape[2] * lax.axis_size("tm")
    table = jnp.asarray((table / windows).astype(jnp.bfloat16))
    if all_bins != bins:
        table = lax.dynamic_slice_in_dim(table, lax.axis_index("freq") * bins, bins, 1)
    table = jnp.transpose(table.reshape(2, CHUNKS, bins // CHUNKS, RANK), (1, 3, 0, 2)).reshape(CHUNKS, RANK, -1)
    high = basis.astype(jnp.bfloat16)
    low = (basis - high.astype(np.float64)).astype(jnp.bfloat16)
    basis = jnp.asarray(np.concatenate([high, high, low], axis=0))

    inputs = [pltpu.with_memory_space_constraint(x, pltpu.HBM) for x in (owners, source_rows, spectra)]
    away = pick(*inputs, shards, 4)
    home = pick(*inputs, shards, 0)
    lots = range(LOTS)
    halves = [home[i] + across(away[i], CORE_MASK) for i in lots]
    halves[0], spectra = lax.optimization_barrier((halves[0], spectra))
    arrived = [[across(half[j + 1], mask) for j, mask in enumerate(HOP_MASKS)] for half in halves]
    white = whiten(meta, spectra)
    arrived[0], white = lax.optimization_barrier((arrived[0], white))
    totals = []
    for half, parts in zip(halves, arrived):
        total = half[0]
        for part in parts:
            total = total + part
        totals.append(total)
    masks = [16 << i for i in range(10) if 16 << i < size] + [12] * (size >= 16)
    for mask in masks[:-1]:
        totals = [total + across(total, mask) for total in totals]
    others = [across(total, masks[-1]) if masks else jnp.zeros_like(total) for total in totals]
    own = [whiten_sum(total, other) for total, other in zip(totals, others)]
    arrived = [[chunk] + [across(chunk, mask) for mask in HOP_MASKS] for chunk in own]

    every = steps * keep // LOTS
    block = math.gcd(BLOCK, every)
    near, far = (0, 1, 2, 3), (4, 5, 6, 7)
    out = None
    sent, kept = [], []
    for i in lots:
        chunks = stack(arrived[i], [begun] if i else [])
        beside = across(chunks, CORE_MASK)
        low = 0 if i + 1 < LOTS else every
        begun = coefficients(meta, {near: chunks}, None, white, table, low, every * shards - low, jnp.float32)
        blocks = []
        for first in range(0, every, block):
            got = [
                coefficients(
                    meta, {far: beside}, (begun, d * every + first - low), white, table, d * every + first, block,
                    jnp.bfloat16,
                )
                for d in range(1, shards)
            ]
            blocks.append(
                [
                    lax.ppermute(part, ("tm", "freq"), [(m, m ^ (d + 1)) for m in range(shards)])
                    for d, part in enumerate(got)
                ]
            )
        sent.append(blocks)
        if low:
            own = coefficients(meta, {near: chunks, far: beside}, None, white, table, 0, every, jnp.float32)
        else:
            own = coefficients(meta, {far: beside}, (begun, 0), white, table, 0, every, jnp.float32)
        kept.append(own)
    for i in lots:
        size = every if i + 1 < LOTS else block
        for first in range(0, every, size):
            some = sent[i][first // block : (first + size) // block]
            out = to_lags(kept[i], some, basis, i * every + first, first, every * LOTS, out, 1 << 28)
    return out.reshape(steps, keep, 128, LAGS)


def solution(mesh):
    placed = (P(None, "freq", "tm", ("parts", "chan")), P("parts"), P("parts", None))
    return jax.shard_map(
        functools.partial(per_device, mesh.shape["chan"]),
        mesh=mesh,
        in_specs=placed,
        out_specs=P(None, ("tm", "freq"), ("parts", "chan"), None),
        check_vma=False,
    )
```
